128 devices in a mesh: dp: 8 (over z, core), owner: 16 (over y, x).
Axes of the slice: x: 4, y: 4, z: 4, core: 2. Of those that a mesh axis runs over, the one named last changes fastest.
Arguments:
- partials: bfloat16 [8, 64, 1024, 1024], P('dp', None, 'owner'), may hold values from -6 to 6
- owner_blocks: int32 [128, 2], replicated, may hold values from -1 to 63, as said below
- left_root: bfloat16 [128, 2, 1024, 1024], P(('dp', 'owner')), may hold values from -1 to 4
- right_root: bfloat16 [128, 2, 1024, 1024], P(('dp', 'owner')), may hold values from -1 to 4
Outputs:
- left_stat: bfloat16 [128, 2, 1024, 1024], P(('dp', 'owner'))
- right_stat: bfloat16 [128, 2, 1024, 1024], P(('dp', 'owner'))
- update: bfloat16 [64, 1024, 1024], P(None, 'owner', 'dp')
The draws below stay inside these ranges and needn't reach their ends.
Inputs may be any that keep to these rules, and one draw needn't show every extreme that they name: `owner_blocks`: every block number 0 to 63 stands in exactly one slot, and -1 marks an empty slot. The owners of data group d are rows d times the owner count onward, one row per owner; their slots hold exactly 8 blocks together. An owner holds 0 to 2 blocks, and in every data group some owner holds 2.
All inputs are finite; a program needn't handle non-finite values.
Results may differ from the reference program's by a relative error of at most 0.02.
Values may be sent and summed in bfloat16 or wider, within the bound.
No kernel may reach another device: no remote copies, remote signals or barrier semaphores. Data moves between devices by JAX's collectives and lax.ppermute only.
A program may use at most 128 MiB of HBM per device.

```python
import math
import jax
import jax.numpy as jnp
from jax import lax

BLOCK = 1024
CAP = 2
BLK_GRP = 8
NB = 64
N_DP = 8
N_OWNER = 16


def draw_owner_blocks(key, part):
    key = jax.random.fold_in(key, 11)
    score_key, busy_key, block_key = jax.random.split(key, 3)
    group_slots = N_OWNER * CAP
    scores = jax.vmap(lambda sub_key: jax.random.permutation(sub_key, group_slots))(jax.random.split(score_key, N_DP))
    busiest = jax.random.randint(busy_key, (N_DP, 1), 0, N_OWNER)
    owner_of_slot = jnp.arange(group_slots, dtype=jnp.int32) // CAP
    scores = scores.astype(jnp.int32) + group_slots * (owner_of_slot[None, :] == busiest).astype(jnp.int32)
    ranking = jnp.argsort(-scores, axis=1, stable=True)
    position = jnp.argsort(ranking, axis=1, stable=True)
    blocks_of_group = jax.random.permutation(block_key, N_DP * BLK_GRP).reshape(N_DP, BLK_GRP).astype(jnp.int32)
    chosen = jnp.take_along_axis(blocks_of_group, jnp.minimum(position, BLK_GRP - 1), axis=1)
    result = jnp.where(position < BLK_GRP, chosen, -1)
    return result.reshape(N_DP * N_OWNER, CAP).astype(jnp.int32)


def build_root(diagonal, jitter):
    identity = jnp.eye(BLOCK, dtype=jnp.float32)
    symmetric = 0.25 * (jitter + jnp.swapaxes(jitter, -1, -2)) / math.sqrt(BLOCK)
    return (identity * diagonal[..., None] + symmetric).astype(jnp.bfloat16)


def draw_left_root(key, part):
    key = jax.random.fold_in(key, 21)
    diag_key, jitter_key = jax.random.split(key)
    mat_shape = (N_DP * N_OWNER, CAP, BLOCK)
    diagonal = jnp.exp(jax.random.uniform(diag_key, mat_shape, jnp.float32, math.log(0.5), math.log(2.0)))
    jitter = jnp.clip(jax.random.normal(jitter_key, mat_shape + (BLOCK,), jnp.float32), -5.0, 5.0)
    return build_root(diagonal, jitter)


def draw_right_root(key, part):
    key = jax.random.fold_in(key, 37)
    diag_key, jitter_key = jax.random.split(key)
    mat_shape = (N_DP * N_OWNER, CAP, BLOCK)
    diagonal = jnp.exp(jax.random.uniform(diag_key, mat_shape, jnp.float32, math.log(0.5), math.log(2.0)))
    jitter = jnp.clip(jax.random.normal(jitter_key, mat_shape + (BLOCK,), jnp.float32), -5.0, 5.0)
    return build_root(diagonal, jitter)


def spiked(entries, own_key, source, target, parts, factor):
    owner, partner = [(jnp.arange(entries.shape[dim]) // (entries.shape[dim] // parts)).reshape([-1 if axis == dim else 1 for axis in range(entries.ndim)]) for dim in (source, target)]
    chosen = jax.random.permutation(own_key, parts)[partner]
    strong = (owner == chosen) | (owner == (partner + parts // 2) % parts)
    return jnp.where(strong, factor * entries, entries)


def levels(rng, shape, cuts, least, largest):
    factor_of, own = 1.0, jax.random.fold_in(rng, 6)
    for dim, shards_of in cuts:
        steps = jnp.exp(jax.random.uniform(jax.random.fold_in(own, dim), (shards_of,), jnp.float32, least / len(cuts), largest / len(cuts)))
        factor_of = factor_of * jnp.repeat(steps, shape[dim] // shards_of).reshape([-1 if axis == dim else 1 for axis in range(len(shape))])
    return factor_of


def gaussian_with(own_key, extent, spread, bound, pieces, heavy, kind=jnp.bfloat16):
    values = spread * jax.random.normal(own_key, extent, jnp.float32)
    if pieces:
        values = values * levels(own_key, extent, pieces, -0.22, 0.18)
    return jnp.clip(spiked(values, jax.random.fold_in(own_key, 3), *heavy), -bound, bound).astype(kind)


def setup_inputs(seed: int = 0) -> dict:
    splits = jax.random.split(jax.random.key(seed), 5)
    partials = gaussian_with(splits[0], (N_DP, NB, BLOCK, BLOCK), 0.35, 6.0, ((0, 8), (2, 16)), (0, 3, 8, 2.0))
    owner_blocks = draw_owner_blocks(jax.random.fold_in(splits[4], 71), 0)
    left_root = draw_left_root(jax.random.fold_in(splits[4], 71), 0)
    right_root = draw_right_root(jax.random.fold_in(splits[4], 71), 0)
    return dict(partials=partials, owner_blocks=owner_blocks, left_root=left_root, right_root=right_root)


def reference(partials, owner_blocks, left_root, right_root):
    blocksize = partials.shape[-1]
    slot_list = owner_blocks.reshape(-1).astype(jnp.int32)
    left_all = left_root.reshape(-1, blocksize, blocksize)
    right_all = right_root.reshape(-1, blocksize, blocksize)

    def slot_work(operands):
        block_id, left_inv, right_inv = operands

        def live_work(unused):
            picked = lax.dynamic_index_in_dim(partials, jnp.maximum(block_id, 0).astype(jnp.int32), 1, keepdims=False)
            gradient = jnp.sum(picked.astype(jnp.float32), axis=0)
            grad_bf = gradient.astype(jnp.bfloat16)
            left_stat = jnp.dot(grad_bf, grad_bf.T, preferred_element_type=jnp.float32) / blocksize
            right_stat = jnp.dot(grad_bf.T, grad_bf, preferred_element_type=jnp.float32) / blocksize
            left_half = jnp.dot(left_inv, grad_bf, preferred_element_type=jnp.float32).astype(jnp.bfloat16)
            updated = jnp.dot(left_half, right_inv, preferred_element_type=jnp.float32)
            return left_stat.astype(jnp.bfloat16), right_stat.astype(jnp.bfloat16), updated.astype(jnp.bfloat16)

        def empty_slot(unused):
            zeros_block = jnp.zeros((blocksize, blocksize), jnp.bfloat16)
            return zeros_block, zeros_block, zeros_block

        return lax.cond(block_id >= 0, live_work, empty_slot, 0)

    left_stat, right_stat, updated = lax.map(slot_work, (slot_list, left_all, right_all))
    nblocks = partials.shape[1]
    is_live = slot_list >= 0
    slot_of_block = jnp.zeros((nblocks,), jnp.int32).at[jnp.where(is_live, slot_list, nblocks)].set(
        jnp.arange(slot_list.shape[0], dtype=jnp.int32), mode="drop")
    update = jnp.take(updated, slot_of_block, axis=0)
    return (left_stat.reshape(left_root.shape), right_stat.reshape(right_root.shape), update)
```

```python
import jax
import jax.numpy as jnp
from jax import lax
from jax.experimental import pallas as pl
from jax.experimental.pallas import tpu as pltpu
from jax.sharding import Mesh, PartitionSpec as P

SPLITS = (256, 256, 512)
GROUPS = 8
NBLOCKS = 64
F32 = jnp.float32
BF16 = jnp.bfloat16
VMEM = pl.BlockSpec(memory_space=pltpu.VMEM)
SMEM = pl.BlockSpec(memory_space=pltpu.SMEM)
HBM = pl.BlockSpec(memory_space=pltpu.HBM)


def params(mebibytes):
    return pltpu.CompilerParams(vmem_limit_bytes=mebibytes * 1024 * 1024)


def cost(flops, nbytes):
    return pl.CostEstimate(flops=flops, bytes_accessed=nbytes, transcendentals=0)


def shape(*dims):
    return jax.ShapeDtypeStruct(dims, BF16)


def add(*terms):
    total = terms[0].astype(F32)
    for term in terms[1:]:
        total = total + term.astype(F32)
    return total.astype(BF16)


def wanted(core):
    low, high = range(4), range(4, 8)
    z = lax.axis_index("z")
    places = []
    for shift, ranks in ((2, low), (1, high), (2, high), (3, low), (1, low), (3, high), (0, low), (0, high)):
        group = lax.rem(z + shift, 4) * 2 + core
        places += [group * 9 + rank for rank in ranks]
    return places


def block_table(owner_blocks, blocks):
    rank = [jnp.int32(0)] * GROUPS
    for slot in range(32):
        for g in range(GROUPS):
            block = owner_blocks[slot % 2, g * 16 + slot // 2]
            blocks[g * 9 + rank[g]] = block
            rank[g] = rank[g] + (block >= 0).astype(jnp.int32)


def copy_blocks(blocks, core, part_ref, outs, sems):
    numbers = [blocks[place] for place in wanted(core)]
    first = 0
    copies = []
    for k, out in enumerate(outs):
        columns = pl.ds(first, out.shape[-1])
        for j, block in enumerate(numbers):
            pltpu.make_async_copy(part_ref.at[block, :, columns], out.at[j], sems.at[k]).start()
        copies.append(pltpu.make_async_copy(part_ref.at[pl.ds(0, 32), :, columns], out, sems.at[k]))
        first += out.shape[-1]
    for copy in copies:
        copy.wait()


def gather_partner(owner_blocks, partials):
    rows, size = partials.shape[1:]

    def body(table_ref, part_ref, blocks, *refs):
        block_table(table_ref, blocks)
        copy_blocks(blocks, 1 - lax.axis_index("core"), part_ref, refs[:-1], refs[-1])

    return pl.pallas_call(
        body,
        in_specs=[SMEM, HBM],
        out_specs=[SMEM, VMEM, VMEM],
        out_shape=[jax.ShapeDtypeStruct((GROUPS * 9,), jnp.int32)]
        + [shape(32, rows, w) for w in (SPLITS[0], size - SPLITS[0])],
        scratch_shapes=[pltpu.SemaphoreType.DMA((2,))],
        compiler_params=params(48),
        cost_estimate=cost(0, 2 * 32 * rows * size * 2),
        name="gather_partner",
    )(owner_blocks, partials)


def gather_own(blocks, partials):
    rows, size = partials.shape[1:]

    def body(block_ref, part_ref, *refs):
        copy_blocks(block_ref, lax.axis_index("core"), part_ref, refs[:-1], refs[-1])

    return pl.pallas_call(
        body,
        in_specs=[SMEM, HBM],
        out_specs=[VMEM] * len(SPLITS),
        out_shape=[shape(32, rows, w) for w in SPLITS],
        scratch_shapes=[pltpu.SemaphoreType.DMA((len(SPLITS),))],
        compiler_params=params(44),
        cost_estimate=cost(0, 2 * 32 * rows * size * 2),
        name="gather_own",
    )(blocks, partials)


def add_pair(own, received, first):
    _, rows, width = own.shape

    def body(own_ref, got_ref, *outs):
        for which, out in enumerate(outs):
            for t in range(8):
                j = 8 * which + t
                out[t] = add(own_ref[j], got_ref[j, :, first : first + width])

    return pl.pallas_call(
        body,
        in_specs=[VMEM, VMEM],
        out_specs=[VMEM] * 4,
        out_shape=[shape(8, rows, width)] * 4,
        compiler_params=params(16),
        cost_estimate=cost(0, 3 * 32 * rows * width * 2),
        name="add_core_pair",
    )(own, received)


def add_waiting(waiting, got_up, got_down):
    _, rows, width = waiting.shape

    def body(wait_ref, up_ref, down_ref, up_out, down_out):
        for t in range(4):
            up_out[t] = add(wait_ref[t], up_ref[t])
            down_out[t] = add(wait_ref[4 + t], down_ref[t])

    return pl.pallas_call(
        body,
        in_specs=[VMEM] * 3,
        out_specs=[VMEM] * 2,
        out_shape=[shape(4, rows, width)] * 2,
        compiler_params=params(16),
        cost_estimate=cost(0, 24 * rows * width * 2),
        name="add_waiting",
    )(waiting, got_up, got_down)


def add_last_and_pick(owner_blocks, chunks):
    rows = chunks[0][0].shape[1]
    widths = [chunk[0].shape[2] for chunk in chunks]

    def body(table_ref, *refs):
        ins, (out_ref, total, sem) = refs[:-3], refs[-3:]
        first = 0
        for k, width in enumerate(widths):
            own_ref, up_ref, down_ref, late_up_ref, late_down_ref = ins[5 * k : 5 * k + 5]
            columns = slice(first, first + width)
            for t in range(4):
                total[t, :, columns] = add(own_ref[t], late_up_ref[t], down_ref[4 + t])
                total[4 + t, :, columns] = add(own_ref[4 + t], late_down_ref[t], up_ref[4 + t])
            first += width
        start = (lax.axis_index("z") * 2 + lax.axis_index("core")) * 16
        rank = jnp.int32(0)
        for slot in range(32):
            pltpu.make_async_copy(
                total.at[jnp.minimum(rank, 7)], out_ref.at[slot // 2, slot % 2], sem
            ).start()
            rank = rank + (table_ref[slot % 2, start + slot // 2] >= 0).astype(jnp.int32)
        pltpu.make_async_copy(out_ref, out_ref, sem).wait()

    return pl.pallas_call(
        body,
        in_specs=[SMEM] + [VMEM] * (5 * len(chunks)),
        out_specs=HBM,
        out_shape=shape(16, 2, rows, sum(widths)),
        scratch_shapes=[pltpu.VMEM((8, rows, sum(widths)), BF16), pltpu.SemaphoreType.DMA],
        compiler_params=params(16),
        cost_estimate=cost(0, 56 * rows * sum(widths) * 2),
        name="add_last_and_pick",
    )(owner_blocks, *[array for chunk in chunks for array in chunk])


def left_product(left_root, arrived):
    owners, slots, rows, width = arrived.shape
    size = owners * rows

    def body(left_ref, grad_ref, out_ref):
        grad = grad_ref[:, 0].reshape(size, width)
        out_ref[0] = jnp.dot(left_ref[0], grad, preferred_element_type=F32).astype(BF16)

    return pl.pallas_call(
        body,
        grid=(slots,),
        in_specs=[
            pl.BlockSpec((1, size, size), lambda c: (c, 0, 0)),
            pl.BlockSpec((owners, 1, rows, width), lambda c: (0, c, 0, 0)),
        ],
        out_specs=pl.BlockSpec((1, size, width), lambda c: (c, 0, 0)),
        out_shape=shape(slots, size, width),
        compiler_params=params(24),
        cost_estimate=cost(2 * slots * size * size * width, 2 * slots * size * (size + 2 * width)),
        name="left_product",
    )(left_root, arrived)


def finish_update(left_root, right_root, left_part, arrived):
    owners, slots, rows, width = arrived.shape
    size = owners * rows
    done = size - width
    tile, col = 256, 128
    cuts = [(at, min(tile, width - at)) for at in range(0, width, tile)]
    per = tile // col

    def body(left_ref, right_ref, part_ref, grad_ref, out_ref, left, right, part, grad, half, out, sems, out_sem):
        copies = {}

        def fetch(name, source, target):
            copies[name] = pltpu.make_async_copy(source, target, sems.at[len(copies)])
            copies[name].start()

        for c in range(slots):
            fetch((c, "left"), left_ref.at[c], left.at[c])
            fetch((c, "grad"), grad_ref.at[:, c], grad.at[c])
            fetch((c, "part"), part_ref.at[c], part.at[c])
            fetch((c, "right"), right_ref.at[c], right.at[c])
        for c in range(slots):
            for name in ("left", "grad"):
                copies[c, name].wait()
            for n, (at, wide) in enumerate(cuts):
                half[:, done + at : done + at + wide] = jnp.dot(
                    left[c], grad[c, :, :, at : at + wide].reshape(size, wide), preferred_element_type=F32
                ).astype(BF16)
            for name in ("part", "right"):
                copies[c, name].wait()
            half[:, :done] = part[c]
            for n in range(size // tile):
                total = jnp.dot(
                    half[...], right[c, :, n * tile : (n + 1) * tile], preferred_element_type=F32
                ).astype(BF16)
                for t in range(per):
                    out[n * per + t, :, c] = total[:, t * col : (t + 1) * col].reshape(owners, rows, col)
                pieces = pl.ds(n * per, per)
                pltpu.make_async_copy(out.at[pieces, :, c], out_ref.at[pieces, :, c], out_sem).start()
        pltpu.make_async_copy(out, out_ref, out_sem).wait()

    return pl.pallas_call(
        body,
        in_specs=[HBM] * 4,
        out_specs=HBM,
        out_shape=shape(size // col, owners, slots, rows, col),
        scratch_shapes=[
            pltpu.VMEM((slots, size, size), BF16),
            pltpu.VMEM((slots, size, size), BF16),
            pltpu.VMEM((slots, size, done), BF16),
            pltpu.VMEM((slots, owners, rows, width), BF16),
            pltpu.VMEM((size, size), BF16),
            pltpu.VMEM((size // col, owners, slots, rows, col), BF16),
            pltpu.SemaphoreType.DMA((4 * slots,)),
            pltpu.SemaphoreType.DMA,
        ],
        compiler_params=params(59),
        cost_estimate=cost(2 * slots * size * size * (width + size), 6 * slots * size * size),
        name="finish_update",
    )(left_root, right_root, left_part, arrived)


def gram_products(owner_blocks, arrived):
    owners, slots, rows, _ = arrived[0].shape
    size = owners * rows
    tile = 256
    count = len(arrived)

    def body(table_ref, *refs):
        parts, (left_out, right_out, places, grad) = refs[:count], refs[count:]
        slot, m = pl.program_id(0), pl.program_id(1)
        me = (lax.axis_index("z") * 2 + lax.axis_index("core")) * owners + lax.axis_index("owner")
        live = table_ref[slot, me] >= 0

        @pl.when((slot == 0) & (m == 0))
        def _():
            for q in range(GROUPS * owners):
                for c in range(slots):
                    block = table_ref[c, q]
                    places[jnp.where(block >= 0, block, NBLOCKS)] = q * slots + c

        @pl.when(m == 0)
        def _():
            first = 0
            for part in parts:
                width = part.shape[-1]
                grad[:, first : first + width] = part[:, 0].reshape(size, width)
                first += width

        at = pl.ds(pl.multiple_of(m * tile, tile), tile)
        left = lax.dot_general(grad[at, :], grad[...], (((1,), (1,)), ((), ())), preferred_element_type=F32)
        right = lax.dot_general(grad[:, at], grad[...], (((0,), (0,)), ((), ())), preferred_element_type=F32)
        left_out[0] = jnp.where(live, left / size, 0.0).astype(BF16)
        right_out[0] = jnp.where(live, right / size, 0.0).astype(BF16)

    out = pl.BlockSpec((1, tile, size), lambda c, m: (c, m, 0))
    return pl.pallas_call(
        body,
        grid=(slots, size // tile),
        in_specs=[SMEM]
        + [pl.BlockSpec((owners, 1, rows, part.shape[-1]), lambda c, m: (0, c, 0, 0)) for part in arrived],
        out_specs=[out, out, SMEM],
        out_shape=[shape(slots, size, size)] * 2 + [jax.ShapeDtypeStruct((NBLOCKS + 1,), jnp.int32)],
        scratch_shapes=[pltpu.VMEM((size, size), BF16)],
        compiler_params=params(24),
        cost_estimate=cost(4 * slots * size**3, 6 * slots * size * size),
        name="gram_products",
    )(owner_blocks, *arrived)


def collect_update(places, received):
    owners, slots, rows, col = received.shape

    def body(place_ref, got_ref, out_ref):
        for block in range(NBLOCKS):
            out_ref[block] = got_ref[place_ref[block]]

    return pl.pallas_call(
        body,
        in_specs=[SMEM, VMEM],
        out_specs=VMEM,
        out_shape=shape(NBLOCKS, rows, col),
        compiler_params=params(16),
        cost_estimate=cost(0, 4 * NBLOCKS * rows * col * 2),
        name="collect_update",
    )(places, received.reshape(owners * slots, rows, col))


def local(partials, owner_blocks, left_root, right_root):
    partials = partials[0]
    left_root, right_root = left_root[0], right_root[0]
    _, rows, size = partials.shape
    owners = size // rows
    table = owner_blocks.T

    swap = [(0, 1), (1, 0)]
    up = [(z, (z + 1) % 4) for z in range(4)]
    down = [(z, (z - 1) % 4) for z in range(4)]

    def along_z(pair):
        return lax.ppermute(pair[0], "z", up), lax.ppermute(pair[1], "z", down)

    blocks, outgoing, outgoing_rest = gather_partner(table, partials)
    received = lax.ppermute(outgoing, "core", swap)
    own = gather_own(blocks, partials)
    outgoing_rest, received, own = lax.optimization_barrier((outgoing_rest, received, own))
    received_rest = lax.ppermute(outgoing_rest, "core", swap)

    def after(array, *earlier):
        return lax.optimization_barrier((array, *earlier))[0]

    *pair_a, wait_a, stay_a = add_pair(own[0], received, 0)
    got_a = along_z(pair_a)
    *pair_b, wait_b, stay_b = add_pair(after(own[1], stay_a), received_rest, 0)
    got_b = along_z(pair_b)
    late_a = add_waiting(after(wait_a, stay_b), *got_a)
    *pair_c, wait_c, stay_c = add_pair(after(own[2], late_a[0]), received_rest, SPLITS[1])
    late_a = along_z(late_a)
    got_c = along_z(lax.optimization_barrier((*pair_c, *got_b, *late_a)))
    picked_a = add_last_and_pick(table, [(after(stay_a, stay_c), *got_a, *late_a)])
    arrived = [lax.all_to_all(picked_a, "owner", split_axis=0, concat_axis=0, tiled=True)]
    late_b = add_waiting(after(wait_b, picked_a), *got_b)
    late_c = add_waiting(after(wait_c, late_b[0]), *got_c)
    late_b, late_c = along_z(late_b), along_z(late_c)
    picked = add_last_and_pick(table, [(stay_b, *got_b, *late_b), (stay_c, *got_c, *late_c)])
    arrived.append(lax.all_to_all(picked, "owner", split_axis=0, concat_axis=0, tiled=True))

    left_part = left_product(left_root, arrived[0])
    pieces = finish_update(left_root, right_root, left_part, arrived[1])
    pieces, arrived = lax.optimization_barrier((pieces, arrived))
    pieces = pieces.reshape(GROUPS * owners, 2, rows, 128)
    received = lax.all_to_all(pieces, ("z", "core", "owner"), split_axis=0, concat_axis=0, tiled=True)
    left_stat, right_stat, places = gram_products(table, arrived)
    update = collect_update(places, received)
    return left_stat[None], right_stat[None], update


def solution(mesh):
    mesh = Mesh(mesh.devices.reshape(4, 2, 16), ("z", "core", "owner"))
    dp = ("z", "core")
    owners = P(("z", "core", "owner"), None, None, None)
    in_specs = (P(dp, None, "owner", None), P(), owners, owners)
    out_specs = (owners, owners, P(None, "owner", dp))
    return jax.shard_map(local, mesh=mesh, in_specs=in_specs, out_specs=out_specs, check_vma=False)
```

```python
import jax
import jax.numpy as jnp
from jax import lax
from jax.experimental import pallas as pl
from jax.experimental.pallas import tpu as pltpu
from jax.sharding import Mesh, PartitionSpec as P

SPLITS = (256, 384, 384)
TILE = 128
GROUPS = 8
NBLOCKS = 64
F32 = jnp.float32
BF16 = jnp.bfloat16
VMEM = pl.BlockSpec(memory_space=pltpu.VMEM)
SMEM = pl.BlockSpec(memory_space=pltpu.SMEM)
HBM = pl.BlockSpec(memory_space=pltpu.HBM)


def params(mebibytes):
    return pltpu.CompilerParams(vmem_limit_bytes=mebibytes * 1024 * 1024)


def cost(flops, nbytes):
    return pl.CostEstimate(flops=flops, bytes_accessed=nbytes, transcendentals=0)


def shape(*dims):
    return jax.ShapeDtypeStruct(dims, BF16)


def add(*terms):
    total = terms[0].astype(F32)
    for term in terms[1:]:
        total = total + term.astype(F32)
    return total.astype(BF16)


def wanted(core):
    low, high = range(4), range(4, 8)
    z = lax.axis_index("z")
    places = []
    for shift, ranks in ((2, low), (1, high), (2, high), (3, low), (1, low), (3, high), (0, low), (0, high)):
        group = lax.rem(z + shift, 4) * 2 + core
        places += [group * 9 + rank for rank in ranks]
    return places


def block_table(owner_blocks, blocks):
    rank = [jnp.int32(0)] * GROUPS
    for slot in range(32):
        for g in range(GROUPS):
            block = owner_blocks[slot % 2, g * 16 + slot // 2]
            blocks[g * 9 + rank[g]] = block
            rank[g] = rank[g] + (block >= 0).astype(jnp.int32)


def copy_blocks(blocks, core, part_ref, first, outs, sems):
    numbers = [blocks[place] for place in wanted(core)]
    copies = []
    for k, out in enumerate(outs):
        columns = pl.ds(first, out.shape[-1])
        for j, block in enumerate(numbers):
            pltpu.make_async_copy(part_ref.at[block, :, columns], out.at[j], sems.at[k]).start()
        copies.append(pltpu.make_async_copy(part_ref.at[pl.ds(0, 32), :, columns], out, sems.at[k]))
        first += out.shape[-1]
    return copies


def gather_first(owner_blocks, partials):
    rows = partials.shape[1]

    def body(table_ref, part_ref, blocks, out, sems):
        block_table(table_ref, blocks)
        for copy in copy_blocks(blocks, 1 - lax.axis_index("core"), part_ref, 0, [out], sems):
            copy.wait()

    return pl.pallas_call(
        body,
        in_specs=[SMEM, HBM],
        out_specs=[SMEM, VMEM],
        out_shape=[jax.ShapeDtypeStruct((GROUPS * 9,), jnp.int32), shape(32, rows, SPLITS[0])],
        scratch_shapes=[pltpu.SemaphoreType.DMA((1,))],
        compiler_params=params(50),
        cost_estimate=cost(0, 2 * 32 * rows * SPLITS[0] * 2),
        name="gather_first",
    )(owner_blocks, partials)


def gather_rest(blocks, partials):
    rows, size = partials.shape[1:]
    widths = (*SPLITS, size - SPLITS[0])

    def body(block_ref, part_ref, *refs):
        *own, other, sems = refs
        core = lax.axis_index("core")
        copies = copy_blocks(block_ref, core, part_ref, 0, own, sems)
        copies += copy_blocks(block_ref, 1 - core, part_ref, SPLITS[0], [other], sems.at[pl.ds(len(own), 1)])
        for copy in copies:
            copy.wait()

    return pl.pallas_call(
        body,
        in_specs=[SMEM, HBM],
        out_specs=[VMEM] * len(widths),
        out_shape=[shape(32, rows, w) for w in widths],
        scratch_shapes=[pltpu.SemaphoreType.DMA((len(widths),))],
        compiler_params=params(44),
        cost_estimate=cost(0, 2 * 32 * rows * sum(widths) * 2),
        name="gather_rest",
    )(blocks, partials)


def add_pair(own, received, first):
    _, rows, width = own.shape

    def body(own_ref, got_ref, *outs):
        for which, out in enumerate(outs):
            for t in range(8):
                j = 8 * which + t
                out[t] = add(own_ref[j], got_ref[j, :, first : first + width])

    return pl.pallas_call(
        body,
        in_specs=[VMEM, VMEM],
        out_specs=[VMEM] * 4,
        out_shape=[shape(8, rows, width)] * 4,
        compiler_params=params(16),
        cost_estimate=cost(0, 3 * 32 * rows * width * 2),
        name="add_core_pair",
    )(own, received)


def cols(tile):
    return slice(tile * TILE, (tile + 1) * TILE)


def mix_first_second(waiting, got_up, got_down, own, received):
    _, rows, width = own.shape
    late, tiles = waiting.shape[2] // TILE, width // TILE
    head = 4 * late

    def body(wait_ref, up_ref, down_ref, own_ref, got_ref, up_out, down_out, wait_out, stay_out):
        for t in range(4):
            for n in range(late):
                up_out[late * t + n] = add(wait_ref[t, :, cols(n)], up_ref[t, :, cols(n)])
                down_out[late * t + n] = add(wait_ref[4 + t, :, cols(n)], down_ref[t, :, cols(n)])
        for t in range(8):
            for n in range(tiles):
                up_out[head + tiles * t + n] = add(own_ref[t, :, cols(n)], got_ref[t, :, cols(n)])
                down_out[head + tiles * t + n] = add(own_ref[8 + t, :, cols(n)], got_ref[8 + t, :, cols(n)])
            wait_out[t] = add(own_ref[16 + t], got_ref[16 + t, :, :width])
            stay_out[t] = add(own_ref[24 + t], got_ref[24 + t, :, :width])

    mixed = shape(head + 8 * tiles, rows, TILE)
    return pl.pallas_call(
        body,
        in_specs=[VMEM] * 5,
        out_specs=[VMEM] * 4,
        out_shape=[mixed, mixed, shape(8, rows, width), shape(8, rows, width)],
        compiler_params=params(16),
        cost_estimate=cost(0, 3 * 32 * rows * width * 2),
        name="mix_first_second",
    )(waiting, got_up, got_down, own, received)


def add_waiting(wait_b, mixed_up, mixed_down, wait_c, got_up, got_down):
    _, rows, width_b = wait_b.shape
    width_c = wait_c.shape[2]
    tiles = width_b // TILE
    head = mixed_up.shape[0] - 8 * tiles

    def body(b_ref, mixed_up_ref, mixed_down_ref, c_ref, up_ref, down_ref, up_out, down_out):
        for t in range(4):
            for n in range(tiles):
                up_out[t, :, cols(n)] = add(b_ref[t, :, cols(n)], mixed_up_ref[head + tiles * t + n])
                down_out[t, :, cols(n)] = add(b_ref[4 + t, :, cols(n)], mixed_down_ref[head + tiles * t + n])
            up_out[t, :, width_b:] = add(c_ref[t], up_ref[t])
            down_out[t, :, width_b:] = add(c_ref[4 + t], down_ref[t])

    return pl.pallas_call(
        body,
        in_specs=[VMEM] * 6,
        out_specs=[VMEM] * 2,
        out_shape=[shape(4, rows, width_b + width_c)] * 2,
        compiler_params=params(16),
        cost_estimate=cost(10**12, 10**9),
        name="add_waiting",
    )(wait_b, mixed_up, mixed_down, wait_c, got_up, got_down)


def pick_slots(table_ref, total, out_ref, sem):
    start = (lax.axis_index("z") * 2 + lax.axis_index("core")) * 16
    rank = jnp.int32(0)
    for slot in range(32):
        pltpu.make_async_copy(total.at[jnp.minimum(rank, 7)], out_ref.at[slot // 2, slot % 2], sem).start()
        rank = rank + (table_ref[slot % 2, start + slot // 2] >= 0).astype(jnp.int32)
    pltpu.make_async_copy(out_ref, out_ref, sem).wait()


def last_call(body, owner_blocks, arrays, rows, width):
    return pl.pallas_call(
        body,
        in_specs=[SMEM] + [VMEM] * len(arrays),
        out_specs=HBM,
        out_shape=shape(16, 2, rows, width),
        scratch_shapes=[pltpu.VMEM((8, rows, width), BF16), pltpu.SemaphoreType.DMA],
        compiler_params=params(16),
        cost_estimate=cost(0, 56 * rows * width * 2),
        name="add_last_and_pick",
    )(owner_blocks, *arrays)


def last_of_first(owner_blocks, stay, got_up, got_down, mixed_up, mixed_down):
    _, rows, width = stay.shape
    late = width // TILE

    def body(table_ref, own_ref, up_ref, down_ref, mixed_up_ref, mixed_down_ref, out_ref, total, sem):
        for t in range(4):
            for n in range(late):
                at = cols(n)
                total[t, :, at] = add(own_ref[t, :, at], mixed_up_ref[late * t + n], down_ref[4 + t, :, at])
                total[4 + t, :, at] = add(own_ref[4 + t, :, at], mixed_down_ref[late * t + n], up_ref[4 + t, :, at])
        pick_slots(table_ref, total, out_ref, sem)

    return last_call(body, owner_blocks, (stay, got_up, got_down, mixed_up, mixed_down), rows, width)


def last_of_rest(owner_blocks, stay_b, mixed_up, mixed_down, stay_c, got_up, got_down, late_up, late_down):
    _, rows, width = late_up.shape
    width_b = stay_b.shape[2]
    tiles = width_b // TILE
    head = mixed_up.shape[0] - 8 * tiles

    def body(table_ref, b_ref, mixed_up_ref, mixed_down_ref, c_ref, up_ref, down_ref, late_up_ref, late_down_ref,
             out_ref, total, sem):
        for t in range(4):
            for n in range(tiles):
                at, high = cols(n), head + tiles * (4 + t) + n
                total[t, :, at] = add(b_ref[t, :, at], late_up_ref[t, :, at], mixed_down_ref[high])
                total[4 + t, :, at] = add(b_ref[4 + t, :, at], late_down_ref[t, :, at], mixed_up_ref[high])
            total[t, :, width_b:] = add(c_ref[t], late_up_ref[t, :, width_b:], down_ref[4 + t])
            total[4 + t, :, width_b:] = add(c_ref[4 + t], late_down_ref[t, :, width_b:], up_ref[4 + t])
        pick_slots(table_ref, total, out_ref, sem)

    arrays = (stay_b, mixed_up, mixed_down, stay_c, got_up, got_down, late_up, late_down)
    return last_call(body, owner_blocks, arrays, rows, width)


def left_product(left_root, arrived):
    owners, slots, rows, width = arrived.shape
    size = owners * rows

    def body(left_ref, grad_ref, out_ref):
        grad = grad_ref[:, 0].reshape(size, width)
        out_ref[0] = jnp.dot(left_ref[0], grad, preferred_element_type=F32).astype(BF16)

    return pl.pallas_call(
        body,
        grid=(slots,),
        in_specs=[
            pl.BlockSpec((1, size, size), lambda c: (c, 0, 0)),
            pl.BlockSpec((owners, 1, rows, width), lambda c: (0, c, 0, 0)),
        ],
        out_specs=pl.BlockSpec((1, size, width), lambda c: (c, 0, 0)),
        out_shape=shape(slots, size, width),
        compiler_params=params(24),
        cost_estimate=cost(2 * slots * size * size * width, 2 * slots * size * (size + 2 * width)),
        name="left_product",
    )(left_root, arrived)


def finish_update(left_root, right_root, left_part, arrived):
    owners, slots, rows, width = arrived.shape
    size = owners * rows
    done = size - width
    tile, col = 512, 128
    per = tile // col

    def body(left_ref, right_ref, part_ref, grad_ref, out_ref, left, right, part, grad, half, out, sems, out_sem):
        copies = {}

        def fetch(c, *names):
            pairs = {
                "left": (left_ref.at[c], left.at[c]),
                "grad": (grad_ref.at[:, c], grad.at[c]),
                "part": (part_ref.at[c], part.at[c]),
                "right": (right_ref.at[c], right.at[c]),
            }
            for name in names:
                copies[c, name] = pltpu.make_async_copy(*pairs[name], sems.at[len(copies)])
                copies[c, name].start()

        fetch(0, "left", "grad")
        for c in range(slots):
            copies[c, "left"].wait()
            copies[c, "grad"].wait()
            fetch(c, "part", "right")
            half[:, done:] = jnp.dot(
                left[c], grad[c].reshape(size, width), preferred_element_type=F32
            ).astype(BF16)
            copies[c, "part"].wait()
            half[:, :done] = part[c]
            copies[c, "right"].wait()
            if c + 1 < slots:
                fetch(c + 1, "left", "grad")
            for n in range(size // tile):
                total = jnp.dot(
                    half[...], right[c, :, n * tile : (n + 1) * tile], preferred_element_type=F32
                ).astype(BF16)
                for t in range(per):
                    out[n * per + t, :, c] = total[:, t * col : (t + 1) * col].reshape(owners, rows, col)
                pieces = pl.ds(n * per, per)
                pltpu.make_async_copy(out.at[pieces, :, c], out_ref.at[pieces, :, c], out_sem).start()
        pltpu.make_async_copy(out, out_ref, out_sem).wait()

    return pl.pallas_call(
        body,
        in_specs=[HBM] * 4,
        out_specs=HBM,
        out_shape=shape(size // col, owners, slots, rows, col),
        scratch_shapes=[
            pltpu.VMEM((slots, size, size), BF16),
            pltpu.VMEM((slots, size, size), BF16),
            pltpu.VMEM((slots, size, done), BF16),
            pltpu.VMEM((slots, owners, rows, width), BF16),
            pltpu.VMEM((size, size), BF16),
            pltpu.VMEM((size // col, owners, slots, rows, col), BF16),
            pltpu.SemaphoreType.DMA((4 * slots,)),
            pltpu.SemaphoreType.DMA,
        ],
        compiler_params=params(59),
        cost_estimate=cost(2 * slots * size * size * (width + size), 6 * slots * size * size),
        name="finish_update",
    )(left_root, right_root, left_part, arrived)


def gram_products(owner_blocks, arrived):
    owners, slots, rows, _ = arrived[0].shape
    size = owners * rows
    tile = 256
    count = len(arrived)

    def body(table_ref, *refs):
        parts, (left_out, right_out, places, grad) = refs[:count], refs[count:]
        slot, m = pl.program_id(0), pl.program_id(1)
        me = (lax.axis_index("z") * 2 + lax.axis_index("core")) * owners + lax.axis_index("owner")
        live = table_ref[slot, me] >= 0

        @pl.when((slot == 0) & (m == 0))
        def _():
            for q in range(GROUPS * owners):
                for c in range(slots):
                    block = table_ref[c, q]
                    places[jnp.where(block >= 0, block, NBLOCKS)] = q * slots + c

        @pl.when(m == 0)
        def _():
            first = 0
            for part in parts:
                width = part.shape[-1]
                grad[:, first : first + width] = part[:, 0].reshape(size, width)
                first += width

        at = pl.ds(pl.multiple_of(m * tile, tile), tile)
        left = lax.dot_general(grad[at, :], grad[...], (((1,), (1,)), ((), ())), preferred_element_type=F32)
        right = lax.dot_general(grad[:, at], grad[...], (((0,), (0,)), ((), ())), preferred_element_type=F32)
        left_out[0] = jnp.where(live, left / size, 0.0).astype(BF16)
        right_out[0] = jnp.where(live, right / size, 0.0).astype(BF16)

    out = pl.BlockSpec((1, tile, size), lambda c, m: (c, m, 0))
    return pl.pallas_call(
        body,
        grid=(slots, size // tile),
        in_specs=[SMEM]
        + [pl.BlockSpec((owners, 1, rows, part.shape[-1]), lambda c, m: (0, c, 0, 0)) for part in arrived],
        out_specs=[out, out, SMEM],
        out_shape=[shape(slots, size, size)] * 2 + [jax.ShapeDtypeStruct((NBLOCKS + 1,), jnp.int32)],
        scratch_shapes=[pltpu.VMEM((size, size), BF16)],
        compiler_params=params(24),
        cost_estimate=cost(4 * slots * size**3, 6 * slots * size * size),
        name="gram_products",
    )(owner_blocks, *arrived)


def collect_update(places, received):
    owners, slots, rows, col = received.shape

    def body(place_ref, got_ref, out_ref, sem):
        for block in range(NBLOCKS):
            pltpu.make_async_copy(got_ref.at[place_ref[block]], out_ref.at[block], sem).start()
        pltpu.make_async_copy(got_ref.at[pl.ds(0, NBLOCKS)], out_ref, sem).wait()

    return pl.pallas_call(
        body,
        in_specs=[SMEM, HBM],
        out_specs=VMEM,
        out_shape=shape(NBLOCKS, rows, col),
        scratch_shapes=[pltpu.SemaphoreType.DMA],
        compiler_params=params(59),
        cost_estimate=cost(0, 4 * NBLOCKS * rows * col * 2),
        name="collect_update",
    )(places, received.reshape(owners * slots, rows, col))


def local(partials, owner_blocks, left_root, right_root):
    partials = partials[0]
    left_root, right_root = left_root[0], right_root[0]
    _, rows, size = partials.shape
    owners = size // rows
    table = owner_blocks.T

    swap = [(0, 1), (1, 0)]
    up = [(z, (z + 1) % 4) for z in range(4)]
    down = [(z, (z - 1) % 4) for z in range(4)]

    def along_z(pair):
        return lax.ppermute(pair[0], "z", up), lax.ppermute(pair[1], "z", down)

    blocks, outgoing = gather_first(table, partials)
    received = lax.ppermute(outgoing, "core", swap)
    *own, outgoing_rest = gather_rest(blocks, partials)
    outgoing_rest, received, own = lax.optimization_barrier((outgoing_rest, received, own))
    received_rest = lax.ppermute(outgoing_rest, "core", swap)

    def after(array, *earlier):
        return lax.optimization_barrier((array, *earlier))[0]

    *pair_a, wait_a, stay_a = add_pair(own[0], received, 0)
    got_a = along_z(pair_a)
    *mixed, wait_b, stay_b = mix_first_second(wait_a, *got_a, own[1], received_rest)
    *pair_c, wait_c, stay_c = add_pair(after(own[2], stay_b), received_rest, SPLITS[1])
    mixed = along_z(mixed)
    got_c = along_z(pair_c)
    picked = last_of_first(table, after(stay_a, stay_c), *got_a, *mixed)
    arrived = [lax.all_to_all(picked, "owner", split_axis=0, concat_axis=0, tiled=True)]
    late = along_z(add_waiting(after(wait_b, picked), *mixed, wait_c, *got_c))
    picked = last_of_rest(table, stay_b, *mixed, stay_c, *got_c, *late)
    arrived.append(lax.all_to_all(picked, "owner", split_axis=0, concat_axis=0, tiled=True))

    left_part = left_product(left_root, arrived[0])
    pieces = finish_update(left_root, right_root, left_part, arrived[1])
    pieces, arrived = lax.optimization_barrier((pieces, arrived))
    pieces = pieces.reshape(GROUPS * owners, 2, rows, 128)
    received = lax.all_to_all(pieces, ("z", "core", "owner"), split_axis=0, concat_axis=0, tiled=True)
    left_stat, right_stat, places = gram_products(table, arrived)
    update = collect_update(places, received)
    return left_stat[None], right_stat[None], update


def solution(mesh):
    mesh = Mesh(mesh.devices.reshape(4, 2, 16), ("z", "core", "owner"))
    dp = ("z", "core")
    owners = P(("z", "core", "owner"), None, None, None)
    in_specs = (P(dp, None, "owner", None), P(), owners, owners)
    out_specs = (owners, owners, P(None, "owner", dp))
    return jax.shard_map(local, mesh=mesh, in_specs=in_specs, out_specs=out_specs, check_vma=False)
```

```python
import jax
import jax.numpy as jnp
from jax import lax
from jax.experimental import pallas as pl
from jax.experimental.pallas import tpu as pltpu
from jax.sharding import Mesh, PartitionSpec as P

SPLITS = (256, 384, 384)
TILE = 128
GROUPS = 8
NBLOCKS = 64
F32 = jnp.float32
BF16 = jnp.bfloat16
VMEM = pl.BlockSpec(memory_space=pltpu.VMEM)
SMEM = pl.BlockSpec(memory_space=pltpu.SMEM)
HBM = pl.BlockSpec(memory_space=pltpu.HBM)
ANY = pl.BlockSpec(memory_space=pl.ANY)


def params(mebibytes):
    return pltpu.CompilerParams(vmem_limit_bytes=mebibytes * 1024 * 1024)


def cost(flops, nbytes):
    return pl.CostEstimate(flops=flops, bytes_accessed=nbytes, transcendentals=0)


def shape(*dims):
    return jax.ShapeDtypeStruct(dims, BF16)


def add(*terms):
    total = terms[0].astype(F32)
    for term in terms[1:]:
        total = total + term.astype(F32)
    return total.astype(BF16)


def wanted(core):
    low, high = range(4), range(4, 8)
    z = lax.axis_index("z")
    places = []
    for shift, ranks in ((2, low), (1, high), (2, high), (3, low), (1, low), (3, high), (0, low), (0, high)):
        group = lax.rem(z + shift, 4) * 2 + core
        places += [group * 9 + rank for rank in ranks]
    return places


def block_table(owner_blocks, blocks):
    rank = [jnp.int32(0)] * GROUPS
    for slot in range(32):
        for g in range(GROUPS):
            block = owner_blocks[slot % 2, g * 16 + slot // 2]
            blocks[g * 9 + rank[g]] = block
            rank[g] = rank[g] + (block >= 0).astype(jnp.int32)


def copy_blocks(blocks, core, part_ref, first, outs, sems):
    numbers = [blocks[place] for place in wanted(core)]
    copies = []
    for k, out in enumerate(outs):
        columns = pl.ds(first, out.shape[-1])
        for j, block in enumerate(numbers):
            pltpu.make_async_copy(part_ref.at[block, :, columns], out.at[j], sems.at[k]).start()
        copies.append(pltpu.make_async_copy(part_ref.at[pl.ds(0, 32), :, columns], out, sems.at[k]))
        first += out.shape[-1]
    return copies


def gather_first(owner_blocks, partials):
    rows = partials.shape[1]

    def body(table_ref, part_ref, blocks, out, sems):
        block_table(table_ref, blocks)
        for copy in copy_blocks(blocks, 1 - lax.axis_index("core"), part_ref, 0, [out], sems):
            copy.wait()

    return pl.pallas_call(
        body,
        in_specs=[SMEM, HBM],
        out_specs=[SMEM, VMEM],
        out_shape=[jax.ShapeDtypeStruct((GROUPS * 9,), jnp.int32), shape(32, rows, SPLITS[0])],
        scratch_shapes=[pltpu.SemaphoreType.DMA((1,))],
        compiler_params=params(50),
        cost_estimate=cost(0, 2 * 32 * rows * SPLITS[0] * 2),
        name="gather_first",
    )(owner_blocks, partials)


def gather_rest(blocks, partials):
    rows, size = partials.shape[1:]
    widths = (*SPLITS, size - SPLITS[0])

    def body(block_ref, part_ref, *refs):
        *own, other, sems = refs
        core = lax.axis_index("core")
        copies = copy_blocks(block_ref, core, part_ref, 0, own, sems)
        copies += copy_blocks(block_ref, 1 - core, part_ref, SPLITS[0], [other], sems.at[pl.ds(len(own), 1)])
        for copy in copies:
            copy.wait()

    return pl.pallas_call(
        body,
        in_specs=[SMEM, HBM],
        out_specs=[VMEM] * len(widths),
        out_shape=[shape(32, rows, w) for w in widths],
        scratch_shapes=[pltpu.SemaphoreType.DMA((len(widths),))],
        compiler_params=params(44),
        cost_estimate=cost(0, 2 * 32 * rows * sum(widths) * 2),
        name="gather_rest",
    )(blocks, partials)


def add_pair(own, received, first):
    _, rows, width = own.shape

    def body(own_ref, got_ref, *outs):
        for which, out in enumerate(outs):
            for t in range(8):
                j = 8 * which + t
                out[t] = add(own_ref[j], got_ref[j, :, first : first + width])

    return pl.pallas_call(
        body,
        in_specs=[VMEM, VMEM],
        out_specs=[VMEM] * 4,
        out_shape=[shape(8, rows, width)] * 4,
        compiler_params=params(16),
        cost_estimate=cost(0, 3 * 32 * rows * width * 2),
        name="add_core_pair",
    )(own, received)


def cols(tile):
    return slice(tile * TILE, (tile + 1) * TILE)


def mix_first_second(waiting, got_up, got_down, own, received):
    _, rows, width = own.shape
    late, tiles = waiting.shape[2] // TILE, width // TILE
    head = 4 * late

    def body(wait_ref, up_ref, down_ref, own_ref, got_ref, up_out, down_out, wait_out, stay_out):
        for t in range(4):
            for n in range(late):
                up_out[late * t + n] = add(wait_ref[t, :, cols(n)], up_ref[t, :, cols(n)])
                down_out[late * t + n] = add(wait_ref[4 + t, :, cols(n)], down_ref[t, :, cols(n)])
        for t in range(8):
            for n in range(tiles):
                up_out[head + tiles * t + n] = add(own_ref[t, :, cols(n)], got_ref[t, :, cols(n)])
                down_out[head + tiles * t + n] = add(own_ref[8 + t, :, cols(n)], got_ref[8 + t, :, cols(n)])
            wait_out[t] = add(own_ref[16 + t], got_ref[16 + t, :, :width])
            stay_out[t] = add(own_ref[24 + t], got_ref[24 + t, :, :width])

    mixed = shape(head + 8 * tiles, rows, TILE)
    return pl.pallas_call(
        body,
        in_specs=[VMEM] * 5,
        out_specs=[VMEM] * 4,
        out_shape=[mixed, mixed, shape(8, rows, width), shape(8, rows, width)],
        compiler_params=params(16),
        cost_estimate=cost(0, 3 * 32 * rows * width * 2),
        name="mix_first_second",
    )(waiting, got_up, got_down, own, received)


def add_waiting(wait_b, mixed_up, mixed_down, wait_c, got_up, got_down):
    _, rows, width_b = wait_b.shape
    width_c = wait_c.shape[2]
    tiles = width_b // TILE
    head = mixed_up.shape[0] - 8 * tiles

    def body(b_ref, mixed_up_ref, mixed_down_ref, c_ref, up_ref, down_ref, up_out, down_out):
        for t in range(4):
            for n in range(tiles):
                up_out[t, :, cols(n)] = add(b_ref[t, :, cols(n)], mixed_up_ref[head + tiles * t + n])
                down_out[t, :, cols(n)] = add(b_ref[4 + t, :, cols(n)], mixed_down_ref[head + tiles * t + n])
            up_out[t, :, width_b:] = add(c_ref[t], up_ref[t])
            down_out[t, :, width_b:] = add(c_ref[4 + t], down_ref[t])

    return pl.pallas_call(
        body,
        in_specs=[VMEM] * 6,
        out_specs=[VMEM] * 2,
        out_shape=[shape(4, rows, width_b + width_c)] * 2,
        compiler_params=params(16),
        cost_estimate=cost(10**12, 10**9),
        name="add_waiting",
    )(wait_b, mixed_up, mixed_down, wait_c, got_up, got_down)


def pick_slots(table_ref, total, out_ref, sem):
    start = (lax.axis_index("z") * 2 + lax.axis_index("core")) * 16
    rank = jnp.int32(0)
    for slot in range(32):
        pltpu.make_async_copy(total.at[jnp.minimum(rank, 7)], out_ref.at[slot // 2, slot % 2], sem).start()
        rank = rank + (table_ref[slot % 2, start + slot // 2] >= 0).astype(jnp.int32)
    pltpu.make_async_copy(out_ref, out_ref, sem).wait()


def last_call(body, owner_blocks, arrays, rows, width):
    return pl.pallas_call(
        body,
        in_specs=[SMEM] + [VMEM] * len(arrays),
        out_specs=HBM,
        out_shape=shape(16, 2, rows, width),
        scratch_shapes=[pltpu.VMEM((8, rows, width), BF16), pltpu.SemaphoreType.DMA],
        compiler_params=params(16),
        cost_estimate=cost(0, 56 * rows * width * 2),
        name="add_last_and_pick",
    )(owner_blocks, *arrays)


def last_of_first(owner_blocks, stay, got_up, got_down, mixed_up, mixed_down):
    _, rows, width = stay.shape
    late = width // TILE

    def body(table_ref, own_ref, up_ref, down_ref, mixed_up_ref, mixed_down_ref, out_ref, total, sem):
        for t in range(4):
            for n in range(late):
                at = cols(n)
                total[t, :, at] = add(own_ref[t, :, at], mixed_up_ref[late * t + n], down_ref[4 + t, :, at])
                total[4 + t, :, at] = add(own_ref[4 + t, :, at], mixed_down_ref[late * t + n], up_ref[4 + t, :, at])
        pick_slots(table_ref, total, out_ref, sem)

    return last_call(body, owner_blocks, (stay, got_up, got_down, mixed_up, mixed_down), rows, width)


def last_of_rest(owner_blocks, stay_b, mixed_up, mixed_down, stay_c, got_up, got_down, late_up, late_down):
    _, rows, width = late_up.shape
    width_b = stay_b.shape[2]
    tiles = width_b // TILE
    head = mixed_up.shape[0] - 8 * tiles

    def body(table_ref, b_ref, mixed_up_ref, mixed_down_ref, c_ref, up_ref, down_ref, late_up_ref, late_down_ref,
             out_ref, total, sem):
        for t in range(4):
            for n in range(tiles):
                at, high = cols(n), head + tiles * (4 + t) + n
                total[t, :, at] = add(b_ref[t, :, at], late_up_ref[t, :, at], mixed_down_ref[high])
                total[4 + t, :, at] = add(b_ref[4 + t, :, at], late_down_ref[t, :, at], mixed_up_ref[high])
            total[t, :, width_b:] = add(c_ref[t], late_up_ref[t, :, width_b:], down_ref[4 + t])
            total[4 + t, :, width_b:] = add(c_ref[4 + t], late_down_ref[t, :, width_b:], up_ref[4 + t])
        pick_slots(table_ref, total, out_ref, sem)

    arrays = (stay_b, mixed_up, mixed_down, stay_c, got_up, got_down, late_up, late_down)
    return last_call(body, owner_blocks, arrays, rows, width)


def left_product(left_root, arrived):
    owners, slots, rows, width = arrived.shape
    size = owners * rows

    def body(left_ref, grad_ref, out_ref):
        grad = grad_ref[:, 0].reshape(size, width)
        out_ref[0] = jnp.dot(left_ref[0], grad, preferred_element_type=F32).astype(BF16)

    return pl.pallas_call(
        body,
        grid=(slots,),
        in_specs=[
            pl.BlockSpec((1, size, size), lambda c: (c, 0, 0)),
            pl.BlockSpec((owners, 1, rows, width), lambda c: (0, c, 0, 0)),
        ],
        out_specs=pl.BlockSpec((1, size, width), lambda c: (c, 0, 0)),
        out_shape=shape(slots, size, width),
        compiler_params=params(24),
        cost_estimate=cost(2 * slots * size * size * width, 2 * slots * size * (size + 2 * width)),
        name="left_product",
    )(left_root, arrived)


def finish_update(left_root, right_root, left_part, arrived):
    owners, slots, rows, width = arrived.shape
    size = owners * rows
    done = size - width
    tile, col = 512, 128
    per = tile // col

    def body(left_ref, right_ref, part_ref, grad_ref, out_ref, left, right, part, grad, half, out, sems, out_sem):
        copies = {}

        low, high = slice(0, size // 2), slice(size // 2, size)

        def fetch(c, *names):
            pairs = {
                "low": (left_ref.at[c, pl.ds(0, size // 2)], left.at[c, pl.ds(0, size // 2)]),
                "high": (left_ref.at[c, pl.ds(size // 2, size // 2)], left.at[c, pl.ds(size // 2, size // 2)]),
                "grad": (grad_ref.at[:, c], grad.at[c]),
                "part": (part_ref.at[c], part.at[c]),
                "right": (right_ref.at[c], right.at[c]),
            }
            for name in names:
                copies[c, name] = pltpu.make_async_copy(*pairs[name], sems.at[len(copies)])
                copies[c, name].start()

        fetch(0, "grad", "low", "high")
        for c in range(slots):
            copies[c, "grad"].wait()
            for name, part_rows in (("low", low), ("high", high)):
                copies[c, name].wait()
                if name == "low":
                    fetch(c, "part", "right")
                half[part_rows, done:] = jnp.dot(
                    left[c, part_rows], grad[c].reshape(size, width), preferred_element_type=F32
                ).astype(BF16)
            copies[c, "part"].wait()
            half[:, :done] = part[c]
            copies[c, "right"].wait()
            if c + 1 < slots:
                fetch(c + 1, "grad", "low", "high")
            for n in range(size // tile):
                total = jnp.dot(
                    half[...], right[c, :, n * tile : (n + 1) * tile], preferred_element_type=F32
                ).astype(BF16)
                for t in range(per):
                    out[n * per + t, :, c] = total[:, t * col : (t + 1) * col].reshape(owners, rows, col)
                pieces = pl.ds(n * per, per)
                pltpu.make_async_copy(out.at[pieces, :, c], out_ref.at[pieces, :, c], out_sem).start()
        pltpu.make_async_copy(out, out_ref, out_sem).wait()

    return pl.pallas_call(
        body,
        in_specs=[HBM, HBM, ANY, ANY],
        out_specs=HBM,
        out_shape=shape(size // col, owners, slots, rows, col),
        scratch_shapes=[
            pltpu.VMEM((slots, size, size), BF16),
            pltpu.VMEM((slots, size, size), BF16),
            pltpu.VMEM((slots, size, done), BF16),
            pltpu.VMEM((slots, owners, rows, width), BF16),
            pltpu.VMEM((size, size), BF16),
            pltpu.VMEM((size // col, owners, slots, rows, col), BF16),
            pltpu.SemaphoreType.DMA((5 * slots,)),
            pltpu.SemaphoreType.DMA,
        ],
        compiler_params=params(59),
        cost_estimate=cost(2 * slots * size * size * (width + size), 6 * slots * size * size),
        name="finish_update",
    )(left_root, right_root, left_part, arrived)


def gram_products(owner_blocks, arrived):
    owners, slots, rows, _ = arrived[0].shape
    size = owners * rows
    tile = 256
    count = len(arrived)

    def body(table_ref, *refs):
        parts, (left_out, right_out, places, grad) = refs[:count], refs[count:]
        slot, m = pl.program_id(0), pl.program_id(1)
        me = (lax.axis_index("z") * 2 + lax.axis_index("core")) * owners + lax.axis_index("owner")
        live = table_ref[slot, me] >= 0

        @pl.when((slot == 0) & (m == 0))
        def _():
            for q in range(GROUPS * owners):
                for c in range(slots):
                    block = table_ref[c, q]
                    places[jnp.where(block >= 0, block, NBLOCKS)] = q * slots + c

        @pl.when(m == 0)
        def _():
            first = 0
            for part in parts:
                width = part.shape[-1]
                grad[:, first : first + width] = part[:, 0].reshape(size, width)
                first += width

        at = pl.ds(pl.multiple_of(m * tile, tile), tile)
        left = lax.dot_general(grad[at, :], grad[...], (((1,), (1,)), ((), ())), preferred_element_type=F32)
        right = lax.dot_general(grad[:, at], grad[...], (((0,), (0,)), ((), ())), preferred_element_type=F32)
        left_out[0] = jnp.where(live, left / size, 0.0).astype(BF16)
        right_out[0] = jnp.where(live, right / size, 0.0).astype(BF16)

    out = pl.BlockSpec((1, tile, size), lambda c, m: (c, m, 0))
    return pl.pallas_call(
        body,
        grid=(slots, size // tile),
        in_specs=[SMEM]
        + [pl.BlockSpec((owners, 1, rows, part.shape[-1]), lambda c, m: (0, c, 0, 0)) for part in arrived],
        out_specs=[out, out, SMEM],
        out_shape=[shape(slots, size, size)] * 2 + [jax.ShapeDtypeStruct((NBLOCKS + 1,), jnp.int32)],
        scratch_shapes=[pltpu.VMEM((size, size), BF16)],
        compiler_params=params(24),
        cost_estimate=cost(4 * slots * size**3, 6 * slots * size * size),
        name="gram_products",
    )(owner_blocks, *arrived)


def collect_update(places, received):
    owners, slots, rows, col = received.shape

    def body(place_ref, got_ref, out_ref, sem):
        for block in range(NBLOCKS):
            pltpu.make_async_copy(got_ref.at[place_ref[block]], out_ref.at[block], sem).start()
        pltpu.make_async_copy(got_ref.at[pl.ds(0, NBLOCKS)], out_ref, sem).wait()

    return pl.pallas_call(
        body,
        in_specs=[SMEM, HBM],
        out_specs=VMEM,
        out_shape=shape(NBLOCKS, rows, col),
        scratch_shapes=[pltpu.SemaphoreType.DMA],
        compiler_params=params(59),
        cost_estimate=cost(0, 4 * NBLOCKS * rows * col * 2),
        name="collect_update",
    )(places, received.reshape(owners * slots, rows, col))


def local(partials, owner_blocks, left_root, right_root):
    partials = partials[0]
    left_root, right_root = left_root[0], right_root[0]
    _, rows, size = partials.shape
    owners = size // rows
    table = owner_blocks.T

    swap = [(0, 1), (1, 0)]
    up = [(z, (z + 1) % 4) for z in range(4)]
    down = [(z, (z - 1) % 4) for z in range(4)]

    def along_z(pair):
        return lax.ppermute(pair[0], "z", up), lax.ppermute(pair[1], "z", down)

    blocks, outgoing = gather_first(table, partials)
    received = lax.ppermute(outgoing, "core", swap)
    *own, outgoing_rest = gather_rest(blocks, partials)
    outgoing_rest, received, own = lax.optimization_barrier((outgoing_rest, received, own))
    received_rest = lax.ppermute(outgoing_rest, "core", swap)

    def after(array, *earlier):
        return lax.optimization_barrier((array, *earlier))[0]

    *pair_a, wait_a, stay_a = add_pair(own[0], received, 0)
    got_a = along_z(pair_a)
    *mixed, wait_b, stay_b = mix_first_second(wait_a, *got_a, own[1], received_rest)
    *pair_c, wait_c, stay_c = add_pair(after(own[2], stay_b), received_rest, SPLITS[1])
    mixed = along_z(mixed)
    got_c = along_z(pair_c)
    picked = last_of_first(table, after(stay_a, stay_c), *got_a, *mixed)
    arrived = [lax.all_to_all(picked, "owner", split_axis=0, concat_axis=0, tiled=True)]
    late = along_z(add_waiting(after(wait_b, picked), *mixed, wait_c, *got_c))
    picked = last_of_rest(table, stay_b, *mixed, stay_c, *got_c, *late)
    arrived.append(lax.all_to_all(picked, "owner", split_axis=0, concat_axis=0, tiled=True))

    left_part = left_product(left_root, arrived[0])
    pieces = finish_update(left_root, right_root, left_part, arrived[1])
    pieces, arrived = lax.optimization_barrier((pieces, arrived))
    pieces = pieces.reshape(GROUPS * owners, 2, rows, 128)
    received = lax.all_to_all(pieces, ("z", "core", "owner"), split_axis=0, concat_axis=0, tiled=True)
    left_stat, right_stat, places = gram_products(table, arrived)
    update = collect_update(places, received)
    return left_stat[None], right_stat[None], update


def solution(mesh):
    mesh = Mesh(mesh.devices.reshape(4, 2, 16), ("z", "core", "owner"))
    dp = ("z", "core")
    owners = P(("z", "core", "owner"), None, None, None)
    in_specs = (P(dp, None, "owner", None), P(), owners, owners)
    out_specs = (owners, owners, P(None, "owner", dp))
    return jax.shard_map(local, mesh=mesh, in_specs=in_specs, out_specs=out_specs, check_vma=False)
```

```python
import jax
import jax.numpy as jnp
from jax import lax
from jax.experimental import pallas as pl
from jax.experimental.pallas import tpu as pltpu
from jax.sharding import Mesh, PartitionSpec as P

SPLITS = (256, 256, 512)
TILE = 128
GROUPS = 8
NBLOCKS = 64
F32 = jnp.float32
BF16 = jnp.bfloat16
VMEM = pl.BlockSpec(memory_space=pltpu.VMEM)
SMEM = pl.BlockSpec(memory_space=pltpu.SMEM)
HBM = pl.BlockSpec(memory_space=pltpu.HBM)


def params(mebibytes):
    return pltpu.CompilerParams(vmem_limit_bytes=mebibytes * 1024 * 1024)


def cost(flops, nbytes):
    return pl.CostEstimate(flops=flops, bytes_accessed=nbytes, transcendentals=0)


def shape(*dims):
    return jax.ShapeDtypeStruct(dims, BF16)


def add(*terms):
    total = terms[0].astype(F32)
    for term in terms[1:]:
        total = total + term.astype(F32)
    return total.astype(BF16)


def wanted(core):
    low, high = range(4), range(4, 8)
    z = lax.axis_index("z")
    places = []
    for shift, ranks in ((2, low), (1, high), (2, high), (3, low), (1, low), (3, high), (0, low), (0, high)):
        group = lax.rem(z + shift, 4) * 2 + core
        places += [group * 9 + rank for rank in ranks]
    return places


def block_table(owner_blocks, blocks):
    rank = [jnp.int32(0)] * GROUPS
    for slot in range(32):
        for g in range(GROUPS):
            block = owner_blocks[slot % 2, g * 16 + slot // 2]
            blocks[g * 9 + rank[g]] = block
            rank[g] = rank[g] + (block >= 0).astype(jnp.int32)


def copy_blocks(blocks, core, part_ref, first, outs, sems):
    numbers = [blocks[place] for place in wanted(core)]
    copies = []
    for k, out in enumerate(outs):
        columns = pl.ds(first, out.shape[-1])
        for j, block in enumerate(numbers):
            pltpu.make_async_copy(part_ref.at[block, :, columns], out.at[j], sems.at[k]).start()
        copies.append(pltpu.make_async_copy(part_ref.at[pl.ds(0, 32), :, columns], out, sems.at[k]))
        first += out.shape[-1]
    return copies


def gather_first(owner_blocks, partials):
    rows = partials.shape[1]

    def body(table_ref, part_ref, blocks, out, sems):
        block_table(table_ref, blocks)
        for copy in copy_blocks(blocks, 1 - lax.axis_index("core"), part_ref, 0, [out], sems):
            copy.wait()

    return pl.pallas_call(
        body,
        in_specs=[SMEM, HBM],
        out_specs=[SMEM, VMEM],
        out_shape=[jax.ShapeDtypeStruct((GROUPS * 9,), jnp.int32), shape(32, rows, SPLITS[0])],
        scratch_shapes=[pltpu.SemaphoreType.DMA((1,))],
        compiler_params=params(50),
        cost_estimate=cost(0, 2 * 32 * rows * SPLITS[0] * 2),
        name="gather_first",
    )(owner_blocks, partials)


def gather_rest(blocks, partials):
    rows, size = partials.shape[1:]
    widths = (*SPLITS, size - SPLITS[0])

    def body(block_ref, part_ref, *refs):
        *own, other, sems = refs
        core = lax.axis_index("core")
        copies = copy_blocks(block_ref, core, part_ref, 0, own, sems)
        copies += copy_blocks(block_ref, 1 - core, part_ref, SPLITS[0], [other], sems.at[pl.ds(len(own), 1)])
        for copy in copies:
            copy.wait()

    return pl.pallas_call(
        body,
        in_specs=[SMEM, HBM],
        out_specs=[VMEM] * len(widths),
        out_shape=[shape(32, rows, w) for w in widths],
        scratch_shapes=[pltpu.SemaphoreType.DMA((len(widths),))],
        compiler_params=params(44),
        cost_estimate=cost(0, 2 * 32 * rows * sum(widths) * 2),
        name="gather_rest",
    )(blocks, partials)


def add_pair(own, received, first):
    _, rows, width = own.shape

    def body(own_ref, got_ref, *outs):
        for which, out in enumerate(outs):
            for t in range(8):
                j = 8 * which + t
                out[t] = add(own_ref[j], got_ref[j, :, first : first + width])

    return pl.pallas_call(
        body,
        in_specs=[VMEM, VMEM],
        out_specs=[VMEM] * 4,
        out_shape=[shape(8, rows, width)] * 4,
        compiler_params=params(16),
        cost_estimate=cost(0, 3 * 32 * rows * width * 2),
        name="add_core_pair",
    )(own, received)


def cols(tile):
    return slice(tile * TILE, (tile + 1) * TILE)


def mix_first_second(waiting, got_up, got_down, own, received):
    _, rows, width = own.shape
    late, tiles = waiting.shape[2] // TILE, width // TILE
    head = 4 * late

    def body(wait_ref, up_ref, down_ref, own_ref, got_ref, up_out, down_out, wait_out, stay_out):
        for t in range(4):
            for n in range(late):
                up_out[late * t + n] = add(wait_ref[t, :, cols(n)], up_ref[t, :, cols(n)])
                down_out[late * t + n] = add(wait_ref[4 + t, :, cols(n)], down_ref[t, :, cols(n)])
        for t in range(8):
            for n in range(tiles):
                up_out[head + tiles * t + n] = add(own_ref[t, :, cols(n)], got_ref[t, :, cols(n)])
                down_out[head + tiles * t + n] = add(own_ref[8 + t, :, cols(n)], got_ref[8 + t, :, cols(n)])
            wait_out[t] = add(own_ref[16 + t], got_ref[16 + t, :, :width])
            stay_out[t] = add(own_ref[24 + t], got_ref[24 + t, :, :width])

    mixed = shape(head + 8 * tiles, rows, TILE)
    return pl.pallas_call(
        body,
        in_specs=[VMEM] * 5,
        out_specs=[VMEM] * 4,
        out_shape=[mixed, mixed, shape(8, rows, width), shape(8, rows, width)],
        compiler_params=params(16),
        cost_estimate=cost(0, 3 * 32 * rows * width * 2),
        name="mix_first_second",
    )(waiting, got_up, got_down, own, received)


def add_waiting(wait_b, mixed_up, mixed_down, wait_c, got_up, got_down):
    _, rows, width_b = wait_b.shape
    width_c = wait_c.shape[2]
    tiles = width_b // TILE
    head = mixed_up.shape[0] - 8 * tiles

    def body(b_ref, mixed_up_ref, mixed_down_ref, c_ref, up_ref, down_ref, up_out, down_out):
        for t in range(4):
            for n in range(tiles):
                up_out[t, :, cols(n)] = add(b_ref[t, :, cols(n)], mixed_up_ref[head + tiles * t + n])
                down_out[t, :, cols(n)] = add(b_ref[4 + t, :, cols(n)], mixed_down_ref[head + tiles * t + n])
            up_out[t, :, width_b:] = add(c_ref[t], up_ref[t])
            down_out[t, :, width_b:] = add(c_ref[4 + t], down_ref[t])

    return pl.pallas_call(
        body,
        in_specs=[VMEM] * 6,
        out_specs=[VMEM] * 2,
        out_shape=[shape(4, rows, width_b + width_c)] * 2,
        compiler_params=params(16),
        cost_estimate=cost(10**12, 10**9),
        name="add_waiting",
    )(wait_b, mixed_up, mixed_down, wait_c, got_up, got_down)


def pick_slots(table_ref, total, out_ref, sem):
    start = (lax.axis_index("z") * 2 + lax.axis_index("core")) * 16
    rank = jnp.int32(0)
    for slot in range(32):
        pltpu.make_async_copy(total.at[jnp.minimum(rank, 7)], out_ref.at[slot // 2, slot % 2], sem).start()
        rank = rank + (table_ref[slot % 2, start + slot // 2] >= 0).astype(jnp.int32)
    pltpu.make_async_copy(out_ref, out_ref, sem).wait()


def last_call(body, owner_blocks, arrays, rows, width, estimate):
    return pl.pallas_call(
        body,
        in_specs=[SMEM] + [VMEM] * len(arrays),
        out_specs=HBM,
        out_shape=shape(16, 2, rows, width),
        scratch_shapes=[pltpu.VMEM((8, rows, width), BF16), pltpu.SemaphoreType.DMA],
        compiler_params=params(16),
        cost_estimate=estimate,
        name="add_last_and_pick",
    )(owner_blocks, *arrays)


def last_of_first(owner_blocks, stay, got_up, got_down, mixed_up, mixed_down):
    _, rows, width = stay.shape
    late = width // TILE

    def body(table_ref, own_ref, up_ref, down_ref, mixed_up_ref, mixed_down_ref, out_ref, total, sem):
        for t in range(4):
            for n in range(late):
                at = cols(n)
                total[t, :, at] = add(own_ref[t, :, at], mixed_up_ref[late * t + n], down_ref[4 + t, :, at])
                total[4 + t, :, at] = add(own_ref[4 + t, :, at], mixed_down_ref[late * t + n], up_ref[4 + t, :, at])
        pick_slots(table_ref, total, out_ref, sem)

    estimate = cost(2 * 10**10, 10**8)
    return last_call(body, owner_blocks, (stay, got_up, got_down, mixed_up, mixed_down), rows, width, estimate)


def last_of_rest(owner_blocks, stay_b, mixed_up, mixed_down, stay_c, got_up, got_down, late_up, late_down):
    _, rows, width = late_up.shape
    width_b = stay_b.shape[2]
    tiles = width_b // TILE
    head = mixed_up.shape[0] - 8 * tiles

    def body(table_ref, b_ref, mixed_up_ref, mixed_down_ref, c_ref, up_ref, down_ref, late_up_ref, late_down_ref,
             out_ref, total, sem):
        for t in range(4):
            for n in range(tiles):
                at, high = cols(n), head + tiles * (4 + t) + n
                total[t, :, at] = add(b_ref[t, :, at], late_up_ref[t, :, at], mixed_down_ref[high])
                total[4 + t, :, at] = add(b_ref[4 + t, :, at], late_down_ref[t, :, at], mixed_up_ref[high])
            total[t, :, width_b:] = add(c_ref[t], late_up_ref[t, :, width_b:], down_ref[4 + t])
            total[4 + t, :, width_b:] = add(c_ref[4 + t], late_down_ref[t, :, width_b:], up_ref[4 + t])
        pick_slots(table_ref, total, out_ref, sem)

    arrays = (stay_b, mixed_up, mixed_down, stay_c, got_up, got_down, late_up, late_down)
    return last_call(body, owner_blocks, arrays, rows, width, cost(0, 56 * rows * width * 2))


def left_product(left_root, arrived):
    owners, slots, rows, width = arrived.shape
    size = owners * rows

    def body(left_ref, grad_ref, out_ref):
        grad = grad_ref[:, 0].reshape(size, width)
        out_ref[0] = jnp.dot(left_ref[0], grad, preferred_element_type=F32).astype(BF16)

    return pl.pallas_call(
        body,
        grid=(slots,),
        in_specs=[
            pl.BlockSpec((1, size, size), lambda c: (c, 0, 0)),
            pl.BlockSpec((owners, 1, rows, width), lambda c: (0, c, 0, 0)),
        ],
        out_specs=pl.BlockSpec((1, size, width), lambda c: (c, 0, 0)),
        out_shape=shape(slots, size, width),
        compiler_params=params(24),
        cost_estimate=cost(2 * slots * size * size * width, 2 * slots * size * (size + 2 * width)),
        name="left_product",
    )(left_root, arrived)


def finish_update(left_root, right_root, left_part, arrived):
    owners, slots, rows, width = arrived.shape
    size = owners * rows
    done = size - width
    tile, col = 512, 128
    per = tile // col

    def body(left_ref, right_ref, part_ref, grad_ref, out_ref, left, right, part, grad, half, out, sems, out_sem):
        copies = {}

        def fetch(c, *names):
            pairs = {
                "left": (left_ref.at[c], left.at[c]),
                "grad": (grad_ref.at[:, c], grad.at[c]),
                "part": (part_ref.at[c], part.at[c]),
                "right": (right_ref.at[c], right.at[c]),
            }
            for name in names:
                copies[c, name] = pltpu.make_async_copy(*pairs[name], sems.at[len(copies)])
                copies[c, name].start()

        fetch(0, "left", "grad")
        for c in range(slots):
            copies[c, "left"].wait()
            copies[c, "grad"].wait()
            fetch(c, "part", "right")
            half[:, done:] = jnp.dot(
                left[c], grad[c].reshape(size, width), preferred_element_type=F32
            ).astype(BF16)
            copies[c, "part"].wait()
            half[:, :done] = part[c]
            copies[c, "right"].wait()
            if c + 1 < slots:
                fetch(c + 1, "left", "grad")
            for n in range(size // tile):
                total = jnp.dot(
                    half[...], right[c, :, n * tile : (n + 1) * tile], preferred_element_type=F32
                ).astype(BF16)
                for t in range(per):
                    out[n * per + t, :, c] = total[:, t * col : (t + 1) * col].reshape(owners, rows, col)
                pieces = pl.ds(n * per, per)
                pltpu.make_async_copy(out.at[pieces, :, c], out_ref.at[pieces, :, c], out_sem).start()
        pltpu.make_async_copy(out, out_ref, out_sem).wait()

    return pl.pallas_call(
        body,
        in_specs=[HBM] * 4,
        out_specs=HBM,
        out_shape=shape(size // col, owners, slots, rows, col),
        scratch_shapes=[
            pltpu.VMEM((slots, size, size), BF16),
            pltpu.VMEM((slots, size, size), BF16),
            pltpu.VMEM((slots, size, done), BF16),
            pltpu.VMEM((slots, owners, rows, width), BF16),
            pltpu.VMEM((size, size), BF16),
            pltpu.VMEM((size // col, owners, slots, rows, col), BF16),
            pltpu.SemaphoreType.DMA((4 * slots,)),
            pltpu.SemaphoreType.DMA,
        ],
        compiler_params=params(59),
        cost_estimate=cost(2 * slots * size * size * (width + size), 6 * slots * size * size),
        name="finish_update",
    )(left_root, right_root, left_part, arrived)


def gram_products(owner_blocks, arrived):
    owners, slots, rows, _ = arrived[0].shape
    size = owners * rows
    tile = 256
    count = len(arrived)

    def body(table_ref, *refs):
        parts, (left_out, right_out, places, grad) = refs[:count], refs[count:]
        slot, m = pl.program_id(0), pl.program_id(1)
        me = (lax.axis_index("z") * 2 + lax.axis_index("core")) * owners + lax.axis_index("owner")
        live = table_ref[slot, me] >= 0

        @pl.when((slot == 0) & (m == 0))
        def _():
            for q in range(GROUPS * owners):
                for c in range(slots):
                    block = table_ref[c, q]
                    places[jnp.where(block >= 0, block, NBLOCKS)] = q * slots + c

        @pl.when(m == 0)
        def _():
            first = 0
            for part in parts:
                width = part.shape[-1]
                grad[:, first : first + width] = part[:, 0].reshape(size, width)
                first += width

        at = pl.ds(pl.multiple_of(m * tile, tile), tile)
        left = lax.dot_general(grad[at, :], grad[...], (((1,), (1,)), ((), ())), preferred_element_type=F32)
        right = lax.dot_general(grad[:, at], grad[...], (((0,), (0,)), ((), ())), preferred_element_type=F32)
        left_out[0] = jnp.where(live, left / size, 0.0).astype(BF16)
        right_out[0] = jnp.where(live, right / size, 0.0).astype(BF16)

    out = pl.BlockSpec((1, tile, size), lambda c, m: (c, m, 0))
    return pl.pallas_call(
        body,
        grid=(slots, size // tile),
        in_specs=[SMEM]
        + [pl.BlockSpec((owners, 1, rows, part.shape[-1]), lambda c, m: (0, c, 0, 0)) for part in arrived],
        out_specs=[out, out, SMEM],
        out_shape=[shape(slots, size, size)] * 2 + [jax.ShapeDtypeStruct((NBLOCKS + 1,), jnp.int32)],
        scratch_shapes=[pltpu.VMEM((size, size), BF16)],
        compiler_params=params(24),
        cost_estimate=cost(4 * slots * size**3, 6 * slots * size * size),
        name="gram_products",
    )(owner_blocks, *arrived)


def collect_update(places, received):
    owners, slots, rows, col = received.shape

    def body(place_ref, got_ref, out_ref, sem):
        for block in range(NBLOCKS):
            pltpu.make_async_copy(got_ref.at[place_ref[block]], out_ref.at[block], sem).start()
        pltpu.make_async_copy(got_ref.at[pl.ds(0, NBLOCKS)], out_ref, sem).wait()

    return pl.pallas_call(
        body,
        in_specs=[SMEM, HBM],
        out_specs=VMEM,
        out_shape=shape(NBLOCKS, rows, col),
        scratch_shapes=[pltpu.SemaphoreType.DMA],
        compiler_params=params(59),
        cost_estimate=cost(0, 4 * NBLOCKS * rows * col * 2),
        name="collect_update",
    )(places, received.reshape(owners * slots, rows, col))


def local(partials, owner_blocks, left_root, right_root):
    partials = partials[0]
    left_root, right_root = left_root[0], right_root[0]
    _, rows, size = partials.shape
    owners = size // rows
    table = owner_blocks.T

    swap = [(0, 1), (1, 0)]
    up = [(z, (z + 1) % 4) for z in range(4)]
    down = [(z, (z - 1) % 4) for z in range(4)]

    def along_z(pair):
        return lax.ppermute(pair[0], "z", up), lax.ppermute(pair[1], "z", down)

    blocks, outgoing = gather_first(table, partials)
    received = lax.ppermute(outgoing, "core", swap)
    *own, outgoing_rest = gather_rest(blocks, partials)
    outgoing_rest, received, own = lax.optimization_barrier((outgoing_rest, received, own))
    received_rest = lax.ppermute(outgoing_rest, "core", swap)

    def after(array, *earlier):
        return lax.optimization_barrier((array, *earlier))[0]

    *pair_a, wait_a, stay_a = add_pair(own[0], received, 0)
    got_a = along_z(pair_a)
    *mixed, wait_b, stay_b = mix_first_second(wait_a, *got_a, own[1], received_rest)
    *pair_c, wait_c, stay_c = add_pair(after(own[2], stay_b), received_rest, SPLITS[1])
    mixed = along_z(mixed)
    got_c = along_z(pair_c)
    picked = last_of_first(table, after(stay_a, stay_c), *got_a, *mixed)
    arrived = [lax.all_to_all(picked, "owner", split_axis=0, concat_axis=0, tiled=True)]
    late = along_z(add_waiting(after(wait_b, picked), *mixed, wait_c, *got_c))
    picked = last_of_rest(table, stay_b, *mixed, stay_c, *got_c, *late)
    arrived.append(lax.all_to_all(picked, "owner", split_axis=0, concat_axis=0, tiled=True))

    left_part = left_product(left_root, arrived[0])
    pieces = finish_update(left_root, right_root, left_part, arrived[1])
    pieces, arrived = lax.optimization_barrier((pieces, arrived))
    pieces = pieces.reshape(GROUPS * owners, 2, rows, 128)
    received = lax.all_to_all(pieces, ("z", "core", "owner"), split_axis=0, concat_axis=0, tiled=True)
    left_stat, right_stat, places = gram_products(table, arrived)
    update = collect_update(places, received)
    return left_stat[None], right_stat[None], update


def solution(mesh):
    mesh = Mesh(mesh.devices.reshape(4, 2, 16), ("z", "core", "owner"))
    dp = ("z", "core")
    owners = P(("z", "core", "owner"), None, None, None)
    in_specs = (P(dp, None, "owner", None), P(), owners, owners)
    out_specs = (owners, owners, P(None, "owner", dp))
    return jax.shard_map(local, mesh=mesh, in_specs=in_specs, out_specs=out_specs, check_vma=False)
```

```python
import jax
import jax.numpy as jnp
from jax import lax
from jax.experimental import pallas as pl
from jax.experimental.pallas import tpu as pltpu
from jax.sharding import Mesh, PartitionSpec as P

SPLITS = (256, 384, 384)
TILE = 128
GROUPS = 8
NBLOCKS = 64
F32 = jnp.float32
BF16 = jnp.bfloat16
VMEM = pl.BlockSpec(memory_space=pltpu.VMEM)
SMEM = pl.BlockSpec(memory_space=pltpu.SMEM)
HBM = pl.BlockSpec(memory_space=pltpu.HBM)


def params(mebibytes):
    return pltpu.CompilerParams(vmem_limit_bytes=mebibytes * 1024 * 1024)


def cost(flops, nbytes):
    return pl.CostEstimate(flops=flops, bytes_accessed=nbytes, transcendentals=0)


def shape(*dims):
    return jax.ShapeDtypeStruct(dims, BF16)


def add(*terms):
    total = terms[0].astype(F32)
    for term in terms[1:]:
        total = total + term.astype(F32)
    return total.astype(BF16)


def wanted(core):
    low, high = range(4), range(4, 8)
    z = lax.axis_index("z")
    places = []
    for shift, ranks in ((2, low), (1, high), (2, high), (3, low), (1, low), (3, high), (0, low), (0, high)):
        group = lax.rem(z + shift, 4) * 2 + core
        places += [group * 9 + rank for rank in ranks]
    return places


def block_table(owner_blocks, blocks):
    rank = [jnp.int32(0)] * GROUPS
    for slot in range(32):
        for g in range(GROUPS):
            block = owner_blocks[slot % 2, g * 16 + slot // 2]
            blocks[g * 9 + rank[g]] = block
            rank[g] = rank[g] + (block >= 0).astype(jnp.int32)


def copy_blocks(blocks, core, part_ref, first, outs, sems):
    numbers = [blocks[place] for place in wanted(core)]
    copies = []
    for k, out in enumerate(outs):
        columns = pl.ds(first, out.shape[-1])
        for j, block in enumerate(numbers):
            pltpu.make_async_copy(part_ref.at[block, :, columns], out.at[j], sems.at[k]).start()
        copies.append(pltpu.make_async_copy(part_ref.at[pl.ds(0, 32), :, columns], out, sems.at[k]))
        first += out.shape[-1]
    return copies


def gather_first(owner_blocks, partials):
    rows = partials.shape[1]

    def body(table_ref, part_ref, blocks, out, sems):
        block_table(table_ref, blocks)
        for copy in copy_blocks(blocks, 1 - lax.axis_index("core"), part_ref, 0, [out], sems):
            copy.wait()

    return pl.pallas_call(
        body,
        in_specs=[SMEM, HBM],
        out_specs=[SMEM, VMEM],
        out_shape=[jax.ShapeDtypeStruct((GROUPS * 9,), jnp.int32), shape(32, rows, SPLITS[0])],
        scratch_shapes=[pltpu.SemaphoreType.DMA((1,))],
        compiler_params=params(50),
        cost_estimate=cost(0, 2 * 32 * rows * SPLITS[0] * 2),
        name="gather_first",
    )(owner_blocks, partials)


def gather_rest(blocks, partials):
    rows, size = partials.shape[1:]
    widths = (*SPLITS, size - SPLITS[0])

    def body(block_ref, part_ref, *refs):
        *own, other, sems = refs
        core = lax.axis_index("core")
        copies = copy_blocks(block_ref, core, part_ref, 0, own, sems)
        copies += copy_blocks(block_ref, 1 - core, part_ref, SPLITS[0], [other], sems.at[pl.ds(len(own), 1)])
        for copy in copies:
            copy.wait()

    return pl.pallas_call(
        body,
        in_specs=[SMEM, HBM],
        out_specs=[VMEM] * len(widths),
        out_shape=[shape(32, rows, w) for w in widths],
        scratch_shapes=[pltpu.SemaphoreType.DMA((len(widths),))],
        compiler_params=params(44),
        cost_estimate=cost(0, 2 * 32 * rows * sum(widths) * 2),
        name="gather_rest",
    )(blocks, partials)


def add_pair(own, received, first):
    _, rows, width = own.shape

    def body(own_ref, got_ref, *outs):
        for which, out in enumerate(outs):
            for t in range(8):
                j = 8 * which + t
                out[t] = add(own_ref[j], got_ref[j, :, first : first + width])

    return pl.pallas_call(
        body,
        in_specs=[VMEM, VMEM],
        out_specs=[VMEM] * 4,
        out_shape=[shape(8, rows, width)] * 4,
        compiler_params=params(16),
        cost_estimate=cost(0, 3 * 32 * rows * width * 2),
        name="add_core_pair",
    )(own, received)


def cols(tile):
    return slice(tile * TILE, (tile + 1) * TILE)


def mix_first_second(waiting, got_up, got_down, own, received):
    _, rows, width = own.shape
    late, tiles = waiting.shape[2] // TILE, width // TILE
    head = 4 * late

    def body(wait_ref, up_ref, down_ref, own_ref, got_ref, up_out, down_out, wait_out, stay_out):
        for t in range(4):
            for n in range(late):
                up_out[late * t + n] = add(wait_ref[t, :, cols(n)], up_ref[t, :, cols(n)])
                down_out[late * t + n] = add(wait_ref[4 + t, :, cols(n)], down_ref[t, :, cols(n)])
        for t in range(8):
            for n in range(tiles):
                up_out[head + tiles * t + n] = add(own_ref[t, :, cols(n)], got_ref[t, :, cols(n)])
                down_out[head + tiles * t + n] = add(own_ref[8 + t, :, cols(n)], got_ref[8 + t, :, cols(n)])
            wait_out[t] = add(own_ref[16 + t], got_ref[16 + t, :, :width])
            stay_out[t] = add(own_ref[24 + t], got_ref[24 + t, :, :width])

    mixed = shape(head + 8 * tiles, rows, TILE)
    return pl.pallas_call(
        body,
        in_specs=[VMEM] * 5,
        out_specs=[VMEM] * 4,
        out_shape=[mixed, mixed, shape(8, rows, width), shape(8, rows, width)],
        compiler_params=params(16),
        cost_estimate=cost(0, 3 * 32 * rows * width * 2),
        name="mix_first_second",
    )(waiting, got_up, got_down, own, received)


def add_waiting(wait_b, mixed_up, mixed_down, wait_c, got_up, got_down):
    _, rows, width_b = wait_b.shape
    width_c = wait_c.shape[2]
    tiles = width_b // TILE
    head = mixed_up.shape[0] - 8 * tiles

    def body(b_ref, mixed_up_ref, mixed_down_ref, c_ref, up_ref, down_ref, up_out, down_out):
        for t in range(4):
            for n in range(tiles):
                up_out[t, :, cols(n)] = add(b_ref[t, :, cols(n)], mixed_up_ref[head + tiles * t + n])
                down_out[t, :, cols(n)] = add(b_ref[4 + t, :, cols(n)], mixed_down_ref[head + tiles * t + n])
            up_out[t, :, width_b:] = add(c_ref[t], up_ref[t])
            down_out[t, :, width_b:] = add(c_ref[4 + t], down_ref[t])

    return pl.pallas_call(
        body,
        in_specs=[VMEM] * 6,
        out_specs=[VMEM] * 2,
        out_shape=[shape(4, rows, width_b + width_c)] * 2,
        compiler_params=params(16),
        cost_estimate=cost(10**12, 10**9),
        name="add_waiting",
    )(wait_b, mixed_up, mixed_down, wait_c, got_up, got_down)


def pick_slots(table_ref, total, out_ref, sem):
    start = (lax.axis_index("z") * 2 + lax.axis_index("core")) * 16
    rank = jnp.int32(0)
    for slot in range(32):
        pltpu.make_async_copy(total.at[jnp.minimum(rank, 7)], out_ref.at[slot // 2, slot % 2], sem).start()
        rank = rank + (table_ref[slot % 2, start + slot // 2] >= 0).astype(jnp.int32)
    pltpu.make_async_copy(out_ref, out_ref, sem).wait()


def last_call(body, owner_blocks, arrays, rows, width):
    return pl.pallas_call(
        body,
        in_specs=[SMEM] + [VMEM] * len(arrays),
        out_specs=HBM,
        out_shape=shape(16, 2, rows, width),
        scratch_shapes=[pltpu.VMEM((8, rows, width), BF16), pltpu.SemaphoreType.DMA],
        compiler_params=params(16),
        cost_estimate=cost(0, 56 * rows * width * 2),
        name="add_last_and_pick",
    )(owner_blocks, *arrays)


def last_of_first(owner_blocks, stay, got_up, got_down, mixed_up, mixed_down):
    _, rows, width = stay.shape
    late = width // TILE

    def body(table_ref, own_ref, up_ref, down_ref, mixed_up_ref, mixed_down_ref, out_ref, total, sem):
        for t in range(4):
            for n in range(late):
                at = cols(n)
                total[t, :, at] = add(own_ref[t, :, at], mixed_up_ref[late * t + n], down_ref[4 + t, :, at])
                total[4 + t, :, at] = add(own_ref[4 + t, :, at], mixed_down_ref[late * t + n], up_ref[4 + t, :, at])
        pick_slots(table_ref, total, out_ref, sem)

    return last_call(body, owner_blocks, (stay, got_up, got_down, mixed_up, mixed_down), rows, width)


def last_of_rest(owner_blocks, stay_b, mixed_up, mixed_down, stay_c, got_up, got_down, late_up, late_down):
    _, rows, width = late_up.shape
    width_b = stay_b.shape[2]
    tiles = width_b // TILE
    head = mixed_up.shape[0] - 8 * tiles

    def body(table_ref, b_ref, mixed_up_ref, mixed_down_ref, c_ref, up_ref, down_ref, late_up_ref, late_down_ref,
             out_ref, total, sem):
        for t in range(4):
            for n in range(tiles):
                at, high = cols(n), head + tiles * (4 + t) + n
                total[t, :, at] = add(b_ref[t, :, at], late_up_ref[t, :, at], mixed_down_ref[high])
                total[4 + t, :, at] = add(b_ref[4 + t, :, at], late_down_ref[t, :, at], mixed_up_ref[high])
            total[t, :, width_b:] = add(c_ref[t], late_up_ref[t, :, width_b:], down_ref[4 + t])
            total[4 + t, :, width_b:] = add(c_ref[4 + t], late_down_ref[t, :, width_b:], up_ref[4 + t])
        pick_slots(table_ref, total, out_ref, sem)

    arrays = (stay_b, mixed_up, mixed_down, stay_c, got_up, got_down, late_up, late_down)
    return last_call(body, owner_blocks, arrays, rows, width)


def left_product(left_root, arrived):
    owners, slots, rows, width = arrived.shape
    size = owners * rows

    def body(left_ref, grad_ref, out_ref):
        grad = grad_ref[:, 0].reshape(size, width)
        out_ref[0] = jnp.dot(left_ref[0], grad, preferred_element_type=F32).astype(BF16)

    return pl.pallas_call(
        body,
        grid=(slots,),
        in_specs=[
            pl.BlockSpec((1, size, size), lambda c: (c, 0, 0)),
            pl.BlockSpec((owners, 1, rows, width), lambda c: (0, c, 0, 0)),
        ],
        out_specs=pl.BlockSpec((1, size, width), lambda c: (c, 0, 0)),
        out_shape=shape(slots, size, width),
        compiler_params=params(24),
        cost_estimate=cost(2 * slots * size * size * width, 2 * slots * size * (size + 2 * width)),
        name="left_product",
    )(left_root, arrived)


def finish_update(left_root, right_root, left_part, arrived):
    owners, slots, rows, width = arrived.shape
    size = owners * rows
    done = size - width
    tile, col = 512, 128
    per = tile // col

    def body(left_ref, right_ref, part_ref, grad_ref, out_ref, left, right, part, grad, half, out, sems, out_sem):
        copies = {}

        def fetch(c, *names):
            pairs = {
                "left": (left_ref.at[c], left.at[c]),
                "grad": (grad_ref.at[:, c], grad.at[c]),
                "part": (part_ref.at[c], part.at[c]),
                "right": (right_ref.at[c], right.at[c]),
            }
            for name in names:
                copies[c, name] = pltpu.make_async_copy(*pairs[name], sems.at[len(copies)])
                copies[c, name].start()

        for c in range(slots):
            fetch(c, "left", "grad", "part", "right")
        for c in range(slots):
            copies[c, "left"].wait()
            copies[c, "grad"].wait()
            half[:, done:] = jnp.dot(
                left[c], grad[c].reshape(size, width), preferred_element_type=F32
            ).astype(BF16)
            copies[c, "part"].wait()
            half[:, :done] = part[c]
            copies[c, "right"].wait()
            for n in range(size // tile):
                total = jnp.dot(
                    half[...], right[c, :, n * tile : (n + 1) * tile], preferred_element_type=F32
                ).astype(BF16)
                for t in range(per):
                    out[n * per + t, :, c] = total[:, t * col : (t + 1) * col].reshape(owners, rows, col)
                pieces = pl.ds(n * per, per)
                pltpu.make_async_copy(out.at[pieces, :, c], out_ref.at[pieces, :, c], out_sem).start()
        pltpu.make_async_copy(out, out_ref, out_sem).wait()

    return pl.pallas_call(
        body,
        in_specs=[HBM] * 4,
        out_specs=HBM,
        out_shape=shape(size // col, owners, slots, rows, col),
        scratch_shapes=[
            pltpu.VMEM((slots, size, size), BF16),
            pltpu.VMEM((slots, size, size), BF16),
            pltpu.VMEM((slots, size, done), BF16),
            pltpu.VMEM((slots, owners, rows, width), BF16),
            pltpu.VMEM((size, size), BF16),
            pltpu.VMEM((size // col, owners, slots, rows, col), BF16),
            pltpu.SemaphoreType.DMA((4 * slots,)),
            pltpu.SemaphoreType.DMA,
        ],
        compiler_params=params(59),
        cost_estimate=cost(2 * slots * size * size * (width + size), 6 * slots * size * size),
        name="finish_update",
    )(left_root, right_root, left_part, arrived)


def gram_products(owner_blocks, arrived):
    owners, slots, rows, _ = arrived[0].shape
    size = owners * rows
    tile = 256
    count = len(arrived)

    def body(table_ref, *refs):
        parts, (left_out, right_out, places, grad) = refs[:count], refs[count:]
        slot, m = pl.program_id(0), pl.program_id(1)
        me = (lax.axis_index("z") * 2 + lax.axis_index("core")) * owners + lax.axis_index("owner")
        live = table_ref[slot, me] >= 0

        @pl.when((slot == 0) & (m == 0))
        def _():
            for q in range(GROUPS * owners):
                for c in range(slots):
                    block = table_ref[c, q]
                    places[jnp.where(block >= 0, block, NBLOCKS)] = q * slots + c

        @pl.when(m == 0)
        def _():
            first = 0
            for part in parts:
                width = part.shape[-1]
                grad[:, first : first + width] = part[:, 0].reshape(size, width)
                first += width

        at = pl.ds(pl.multiple_of(m * tile, tile), tile)
        left = lax.dot_general(grad[at, :], grad[...], (((1,), (1,)), ((), ())), preferred_element_type=F32)
        right = lax.dot_general(grad[:, at], grad[...], (((0,), (0,)), ((), ())), preferred_element_type=F32)
        left_out[0] = jnp.where(live, left / size, 0.0).astype(BF16)
        right_out[0] = jnp.where(live, right / size, 0.0).astype(BF16)

    out = pl.BlockSpec((1, tile, size), lambda c, m: (c, m, 0))
    return pl.pallas_call(
        body,
        grid=(slots, size // tile),
        in_specs=[SMEM]
        + [pl.BlockSpec((owners, 1, rows, part.shape[-1]), lambda c, m: (0, c, 0, 0)) for part in arrived],
        out_specs=[out, out, SMEM],
        out_shape=[shape(slots, size, size)] * 2 + [jax.ShapeDtypeStruct((NBLOCKS + 1,), jnp.int32)],
        scratch_shapes=[pltpu.VMEM((size, size), BF16)],
        compiler_params=params(24),
        cost_estimate=cost(4 * slots * size**3, 6 * slots * size * size),
        name="gram_products",
    )(owner_blocks, *arrived)


def collect_update(places, received):
    owners, slots, rows, col = received.shape

    def body(place_ref, got_ref, out_ref, sem):
        for block in range(NBLOCKS):
            pltpu.make_async_copy(got_ref.at[place_ref[block]], out_ref.at[block], sem).start()
        pltpu.make_async_copy(got_ref.at[pl.ds(0, NBLOCKS)], out_ref, sem).wait()

    return pl.pallas_call(
        body,
        in_specs=[SMEM, HBM],
        out_specs=VMEM,
        out_shape=shape(NBLOCKS, rows, col),
        scratch_shapes=[pltpu.SemaphoreType.DMA],
        compiler_params=params(59),
        cost_estimate=cost(0, 4 * NBLOCKS * rows * col * 2),
        name="collect_update",
    )(places, received.reshape(owners * slots, rows, col))


def local(partials, owner_blocks, left_root, right_root):
    partials = partials[0]
    left_root, right_root = left_root[0], right_root[0]
    _, rows, size = partials.shape
    owners = size // rows
    table = owner_blocks.T

    swap = [(0, 1), (1, 0)]
    up = [(z, (z + 1) % 4) for z in range(4)]
    down = [(z, (z - 1) % 4) for z in range(4)]

    def along_z(pair):
        return lax.ppermute(pair[0], "z", up), lax.ppermute(pair[1], "z", down)

    blocks, outgoing = gather_first(table, partials)
    received = lax.ppermute(outgoing, "core", swap)
    *own, outgoing_rest = gather_rest(blocks, partials)
    outgoing_rest, received, own = lax.optimization_barrier((outgoing_rest, received, own))
    received_rest = lax.ppermute(outgoing_rest, "core", swap)

    def after(array, *earlier):
        return lax.optimization_barrier((array, *earlier))[0]

    *pair_a, wait_a, stay_a = add_pair(own[0], received, 0)
    got_a = along_z(pair_a)
    *mixed, wait_b, stay_b = mix_first_second(wait_a, *got_a, own[1], received_rest)
    *pair_c, wait_c, stay_c = add_pair(after(own[2], stay_b), received_rest, SPLITS[1])
    mixed = along_z(mixed)
    got_c = along_z(pair_c)
    picked = last_of_first(table, after(stay_a, stay_c), *got_a, *mixed)
    arrived = [lax.all_to_all(picked, "owner", split_axis=0, concat_axis=0, tiled=True)]
    late = along_z(add_waiting(after(wait_b, picked), *mixed, wait_c, *got_c))
    picked = last_of_rest(table, stay_b, *mixed, stay_c, *got_c, *late)
    arrived.append(lax.all_to_all(picked, "owner", split_axis=0, concat_axis=0, tiled=True))

    left_part = left_product(left_root, arrived[0])
    pieces = finish_update(left_root, right_root, left_part, arrived[1])
    pieces, arrived = lax.optimization_barrier((pieces, arrived))
    pieces = pieces.reshape(GROUPS * owners, 2, rows, 128)
    received = lax.all_to_all(pieces, ("z", "core", "owner"), split_axis=0, concat_axis=0, tiled=True)
    left_stat, right_stat, places = gram_products(table, arrived)
    update = collect_update(places, received)
    return left_stat[None], right_stat[None], update


def solution(mesh):
    mesh = Mesh(mesh.devices.reshape(4, 2, 16), ("z", "core", "owner"))
    dp = ("z", "core")
    owners = P(("z", "core", "owner"), None, None, None)
    in_specs = (P(dp, None, "owner", None), P(), owners, owners)
    out_specs = (owners, owners, P(None, "owner", dp))
    return jax.shard_map(local, mesh=mesh, in_specs=in_specs, out_specs=out_specs, check_vma=False)
```
